32 devices in a mesh: frame: 4 (over y, x), head: 4 (over z), tok: 2 (over core).
Axes of the slice: x: 2, y: 2, z: 4, core: 2. Of those that a mesh axis runs over, the one named last changes fastest.
Arguments:
- queries: bfloat16 [4, 768, 512], P('frame', ('head', 'tok')), may hold values from -120 to 120
- keys: bfloat16 [4, 768, 512], P('frame', ('head', 'tok')), may hold values from -4 to 4
- values: bfloat16 [4, 768, 512], P('frame', ('head', 'tok')), may hold values from -6 to 6
- residual: bfloat16 [4, 768, 512], P('frame', ('head', 'tok')), may hold values from -6 to 6
- incoming: bfloat16 [768, 512], P(('head', 'tok')), may hold values from -6 to 6
- gate_table: float32 [50, 512], replicated, may hold values from -2 to 2
- timesteps: int32 [4], P('frame'), may hold values from 0 to 49
- positions: int32 [4], P('frame'), may hold values from 0 to 9, as said below
Outputs:
- next_queue: bfloat16 [4, 768, 512], P('frame', ('head', 'tok'))
- leaving: bfloat16 [768, 512], P(('head', 'tok'), 'frame')
The draws below stay inside these ranges and needn't reach their ends.
Inputs may be any that keep to these rules, and one draw needn't show every extreme that they name: positions rise strictly along the queue, by 1 to 5 from one frame to the next; the first frame's position is 0 and the last frame's is 9.
All inputs are finite; a program needn't handle non-finite values.
Results may differ from the reference program's by a relative error of at most 0.007.
Values may be sent and summed in bfloat16 or wider, within the bound.
A program may use at most 64 MiB of HBM per device.

```python
import math
import jax
import jax.numpy as jnp
from jax import lax

HD = 128
HEADS = 4
HH = 512
FRAME_TOK = 768
FRAMES = 4
STEPS = 50
ROPE_DIMS = 16


def drawn_base(key):
    array_shape = (FRAMES, FRAME_TOK, HEADS * HD)
    base_keys = jnp.clip(jax.random.normal(jax.random.fold_in(key, 101), array_shape, jnp.float32), -4.0, 4.0)
    return base_keys


def draw_keys(key, part):
    base_keys = drawn_base(key)
    return base_keys.astype(jnp.bfloat16)


def draw_queries(key, part):
    base_keys = drawn_base(key)
    key = jax.random.fold_in(key, 4)
    spread = 2.5 * jnp.clip(jax.random.normal(jax.random.fold_in(key, 1), base_keys.shape, jnp.float32), -4.0, 4.0)
    return spread.astype(jnp.bfloat16)


def draw_positions(key, part):
    key = jax.random.fold_in(key, 5)
    jitter = jax.random.randint(jax.random.fold_in(key, 1), (FRAMES,), 0, 3)
    frame_ids = jnp.arange(FRAMES, dtype=jnp.int32)
    pinned = (frame_ids == 0) | (frame_ids == FRAMES - 1)
    jitter = jnp.where(pinned, 0, jitter)
    return (3 * frame_ids + jitter).astype(jnp.int32)


def with_ends(entries, stream_key, smallest, high):
    longest = entries.shape.index(max(entries.shape))
    spots = []
    for shift in (0, 1):
        where = [jax.random.randint(jax.random.fold_in(stream_key, axis), (), 0, length) for axis, length in enumerate(entries.shape)]
        where[longest] = (where[longest] + shift) % entries.shape[longest]
        spots.append(tuple(where))
    return entries.at[spots[0]].set(smallest).at[spots[1]].set(high)


def level_of(own_key, shape, shards, low, largest):
    loudness, own = 1.0, jax.random.fold_in(own_key, 6)
    for position, shards_of in shards:
        steps = jnp.exp(jax.random.uniform(jax.random.fold_in(own, position), (shards_of,), jnp.float32, low / len(shards), largest / len(shards)))
        loudness = loudness * jnp.repeat(steps, shape[position] // shards_of).reshape([-1 if axis == position else 1 for axis in range(len(shape))])
    return loudness


def centred(own_key, extent, scale, most, split=(), kind=jnp.bfloat16):
    gain = level_of(own_key, extent, split, -0.22, 0.18) if split else 1.0
    result = jax.random.normal(own_key, extent, jnp.float32) * scale * gain
    return jnp.minimum(jnp.maximum(result, -most), most).astype(kind)


def setup_inputs(seed: int = 0) -> dict:
    arg_keys = jax.random.split(jax.random.key(seed), 9)
    return {
        "queries": draw_queries(jax.random.fold_in(arg_keys[8], 71), 0),
        "keys": draw_keys(jax.random.fold_in(arg_keys[8], 71), 0),
        "values": centred(arg_keys[2], (FRAMES, FRAME_TOK, HH), 1.0, 6.0, ((0, 4), (1, 8))),
        "residual": centred(arg_keys[3], (FRAMES, FRAME_TOK, HH), 1.0, 6.0, ((0, 4), (1, 8))),
        "incoming": centred(arg_keys[4], (FRAME_TOK, HH), 1.0, 6.0, ((0, 8),)),
        "gate_table": jnp.clip(jax.random.uniform(arg_keys[5], (STEPS, HH), jnp.float32, -2.0, 2.0), -2.0, 2.0),
        "timesteps": with_ends(jax.random.randint(arg_keys[6], (FRAMES,), 0, STEPS), jax.random.fold_in(arg_keys[6], 1), 0, STEPS - 1).astype(jnp.int32),
        "positions": draw_positions(jax.random.fold_in(arg_keys[8], 71), 0),
    }


rope_base = 256.0

def rotate(block_data, positions):
    frames, tokens, columns_all = block_data.shape
    shaped = block_data.astype(jnp.float32).reshape(frames, tokens, columns_all // HD, HD)
    half_dims = ROPE_DIMS // 2
    frequency = rope_base ** (-jnp.arange(half_dims, dtype=jnp.float32) / half_dims)
    angles = positions.astype(jnp.float32)[:, None, None, None] * frequency
    cosine = jnp.cos(angles)
    sine_term = jnp.sin(angles)
    leading = shaped[..., :half_dims]
    second = shaped[..., half_dims:ROPE_DIMS]
    turned = jnp.concatenate([leading * cosine - second * sine_term, second * cosine + leading * sine_term, shaped[..., ROPE_DIMS:]], axis=-1)
    return turned.reshape(frames, tokens, columns_all).astype(jnp.bfloat16)

def reference(queries, keys, values, residual, incoming, gate_table, timesteps, positions):
    turned_queries = rotate(queries, positions)
    turned_keys = rotate(keys, positions)
    score_scale = 1.0 / math.sqrt(HD)
    offsets = jnp.array([-1, 0, 1], dtype=jnp.int32)

    def one_frame(frame_index):
        nearby = frame_index + offsets
        usable = (nearby >= 0) & (nearby < FRAMES)
        picked = jnp.clip(nearby, 0, FRAMES - 1).astype(jnp.int32)
        near_keys = jnp.take(turned_keys, picked, axis=0).reshape(3 * FRAME_TOK, HH)
        near_values = jnp.take(values, picked, axis=0).reshape(3 * FRAME_TOK, HH)
        key_mask = jnp.repeat(usable, FRAME_TOK)
        own_queries = lax.dynamic_index_in_dim(turned_queries, frame_index, 0, keepdims=False)

        def one_head(head_index):
            start_col = (head_index * HD).astype(jnp.int32)
            head_queries = lax.dynamic_slice_in_dim(own_queries, start_col, HD, 1)
            head_keys = lax.dynamic_slice_in_dim(near_keys, start_col, HD, 1)
            head_values = lax.dynamic_slice_in_dim(near_values, start_col, HD, 1)
            scores = jnp.dot(head_queries, head_keys.T, preferred_element_type=jnp.float32) * score_scale
            scores = jnp.where(key_mask[None, :], scores, -jnp.inf)
            highest = lax.optimization_barrier(jnp.max(scores, axis=1, keepdims=True))
            weights = jnp.exp(scores - highest)
            running_total = lax.optimization_barrier(jnp.sum(weights, axis=1, keepdims=True))
            blended = jnp.dot(weights.astype(jnp.bfloat16), head_values, preferred_element_type=jnp.float32)
            return (blended / running_total).astype(jnp.bfloat16)
        heads_out = lax.map(one_head, jnp.arange(HEADS, dtype=jnp.int32))
        return jnp.transpose(heads_out, (1, 0, 2)).reshape(FRAME_TOK, HH)
    attention = lax.map(one_frame, jnp.arange(FRAMES, dtype=jnp.int32))
    gates = jnp.take(gate_table, timesteps, axis=0)
    updated = (residual.astype(jnp.float32) + gates[:, None, :] * attention.astype(jnp.float32)).astype(jnp.bfloat16)
    next_queue = jnp.concatenate([updated[1:], incoming[None]], axis=0)
    leaving = updated[0]
    return (next_queue, leaving)
```

```python
import functools
import math

import jax
import jax.numpy as jnp
from jax import lax
from jax.experimental import pallas as pl
from jax.experimental.pallas import tpu as pltpu
from jax.sharding import PartitionSpec as P

HD = 128
HALF = 8
MESH = pl.DeviceIdType.MESH
ABSENT = 1e30


def kernel(
    frames, heads, relay,
    q_hbm, k_hbm, v_hbm, res_hbm, inc_hbm, gate_hbm, steps_ref, pos_ref,
    nq_ref, lv_ref,
    q_in, k_in, gate_in, kv_out, q_out, gate_out,
    kv_buf, q_buf, o_out, o_buf, lo_buf, res_buf, lres_buf, gate_buf, lgate_buf, nq_buf, lv_buf,
    load_sem, v_sem, kvz_s, kvz_r, qz_s, qz_r, peer_s, peer_r, fr_s, fr_r, rl_s, fwd_s, fwd_r,
    o_s, o_r, lo_r, res_s, res_r, lres_s, lres_r, gate_s, gate_r, lgate_s, lgate_r, out_sem,
):
    F, Z = frames, heads
    f = lax.axis_index("frame")
    h = lax.axis_index("head")
    t = lax.axis_index("tok")
    T = q_in.shape[0]
    has_prev = f > 0
    has_next = f < F - 1

    def at(fr, hd, tk):
        return {"frame": fr, "head": hd, "tok": tk}

    def remote(src, dst, send, recv, dev):
        return pltpu.make_async_remote_copy(
            src_ref=src, dst_ref=dst, send_sem=send, recv_sem=recv, device_id=dev, device_id_type=MESH
        )

    load_k = pltpu.make_async_copy(k_hbm.at[0], k_in, load_sem.at[0])
    load_q = pltpu.make_async_copy(q_hbm.at[0], q_in, load_sem.at[1])
    load_gate = pltpu.make_async_copy(gate_hbm, gate_in, load_sem.at[2])
    load_v = [
        pltpu.make_async_copy(v_hbm.at[0, :, pl.ds(j * HD, HD)], kv_out.at[j, 1], v_sem.at[j]) for j in range(Z)
    ]
    load_k.start()
    for c in load_v:
        c.start()
    load_q.start()
    load_gate.start()

    barrier = pltpu.get_barrier_semaphore()
    me = f * Z + h

    def greet(s, carry):
        other = lax.rem(me + s, F * Z)
        pl.semaphore_signal(barrier, inc=1, device_id=at(other // Z, lax.rem(other, Z), t), device_id_type=MESH)
        return carry

    lax.fori_loop(1, F * Z, greet, 0)
    pl.semaphore_signal(barrier, inc=1, device_id=at(f, h, 1 - t), device_id_type=MESH)

    lane = lax.broadcasted_iota(jnp.int32, (8, HD), 1)
    power = lax.rem(lane, HALF).astype(jnp.float32)
    angle = pos_ref[0].astype(jnp.float32) * jnp.exp2(-power)
    cosine = jnp.where(lane < 2 * HALF, jnp.cos(angle), 1.0)[0:1]
    sine = jnp.sin(angle)
    sine_up = jnp.where(lane < HALF, -sine, 0.0)[0:1]
    sine_down = jnp.where((lane >= HALF) & (lane < 2 * HALF), sine, 0.0)[0:1]

    def turned(x):
        x = x.astype(jnp.float32)
        up = pltpu.roll(x, HD - HALF, 1)
        down = pltpu.roll(x, HALF, 1)
        return (x * cosine + up * sine_up + down * sine_down).astype(jnp.bfloat16)

    load_k.wait()
    for j in range(Z):
        kv_out[j, 0] = turned(k_in[:, j * HD : (j + 1) * HD])
    load_q.wait()
    for j in range(Z):
        q_out[j] = turned(q_in[:, j * HD : (j + 1) * HD])
    for c in load_v:
        c.wait()
    pl.semaphore_wait(barrier, F * Z)

    def kv_send(s):
        d = lax.rem(h + s, Z)
        return remote(kv_out.at[d], kv_buf.at[0, t, h], kvz_s.at[s], kvz_r.at[s], at(f, d, t))

    def q_send(s):
        d = lax.rem(h + s, Z)
        return remote(q_out.at[d], q_buf.at[h], qz_s.at[s], qz_r.at[s], at(f, d, t))

    for s in range(1, Z):
        kv_send(s).start()

    def peer_send(s, b, src):
        return remote(src, kv_buf.at[0, t, b], peer_s.at[s], peer_r.at[s], at(f, h, 1 - t))

    def next_send(s, b, src):
        return remote(src, kv_buf.at[1, t, b], fr_s.at[0, s], fr_r.at[0, s], at(f + 1, h, t))

    def prev_send(s, b, src):
        return remote(src, kv_buf.at[2, t, b], fr_s.at[1, s], fr_r.at[1, s], at(f - 1, h, t))

    sends_next = has_next
    sends_prev = has_prev
    if relay:
        sends_next = has_next & (f != 1)
        sends_prev = has_prev & (f != 2)

    def spread(s, b, src):
        @pl.when(sends_next)
        def _():
            next_send(s, b, src).start()

        @pl.when(sends_prev)
        def _():
            prev_send(s, b, src).start()

        peer_send(s, b, src).start()

    spread(0, h, kv_out.at[h])
    for s in range(1, Z):
        q_send(s).start()
    kv_buf[0, t, h] = kv_out[h]
    q_buf[h] = q_out[h]

    load_gate.wait()
    gate_out[...] = jnp.broadcast_to(gate_in[pl.ds(steps_ref[0], 1), :], gate_out.shape)

    def res_send():
        return remote(res_hbm, res_buf, res_s, res_r, at(f - 1, h, t))

    def gate_send():
        return remote(gate_out, gate_buf, gate_s, gate_r, at(f - 1, h, t))

    def lres_send(g):
        return remote(res_hbm.at[0, :, pl.ds(g * HD, HD)], lres_buf, lres_s.at[g], lres_r, at(g, h, t))

    def lgate_send(g):
        return remote(gate_out.at[:, pl.ds(g * HD, HD)], lgate_buf, lgate_s.at[g], lgate_r, at(g, h, t))

    @pl.when(has_prev)
    def _():
        res_send().start()
        gate_send().start()

    @pl.when(f == 0)
    def _():
        pltpu.make_async_copy(res_hbm.at[0, :, pl.ds(0, HD)], lres_buf, lres_r).start()
        pltpu.make_async_copy(gate_out.at[:, pl.ds(0, HD)], lgate_buf, lgate_r).start()
        for g in range(1, F):
            lres_send(g).start()
            lgate_send(g).start()
        kv_buf[1] = jnp.zeros(kv_buf.shape[1:], kv_buf.dtype)

    @pl.when(f == F - 1)
    def _():
        kv_buf[2] = jnp.zeros(kv_buf.shape[1:], kv_buf.dtype)

    for s in range(1, Z):
        b = lax.rem(h + Z - s, Z)
        remote(kv_out.at[0], kv_buf.at[0, t, b], kvz_s.at[s], kvz_r.at[s], at(f, b, t)).wait_recv()
        spread(s, b, kv_buf.at[0, t, b])

    def fwd_send(slot, s, b):
        ref = kv_buf.at[slot, t, b]
        return remote(ref, ref, fwd_s.at[slot - 1, s], fwd_r.at[slot - 1, s], at(f, h, 1 - t))

    def relay_down(s, b):
        return remote(kv_buf.at[2, t, b], kv_buf.at[1, t, b], rl_s.at[s], fr_r.at[0, s], at(2, h, t))

    def relay_up(s, b):
        return remote(kv_buf.at[1, t, b], kv_buf.at[2, t, b], rl_s.at[s], fr_r.at[1, s], at(1, h, t))

    for s in range(Z):
        b = lax.rem(h + Z - s, Z)

        @pl.when(has_prev)
        def _():
            remote(kv_out.at[0], kv_buf.at[1, t, b], fr_s.at[0, s], fr_r.at[0, s], at(f, h, 1 - t)).wait_recv()
            if relay:

                @pl.when(f == 3)
                def _():
                    relay_up(s, b).start()

            fwd_send(1, s, b).start()

        @pl.when(has_next)
        def _():
            remote(kv_out.at[0], kv_buf.at[2, t, b], fr_s.at[1, s], fr_r.at[1, s], at(f, h, 1 - t)).wait_recv()
            if relay:

                @pl.when(f == 0)
                def _():
                    relay_down(s, b).start()

            fwd_send(2, s, b).start()

    for s in range(Z):
        b = lax.rem(h + Z - s, Z)
        remote(kv_out.at[0], kv_buf.at[0, 1 - t, b], peer_s.at[s], peer_r.at[s], at(f, h, 1 - t)).wait_recv()
        if s > 0:
            remote(q_out.at[0], q_buf.at[b], qz_s.at[s], qz_r.at[s], at(f, b, t)).wait_recv()

        @pl.when(has_prev)
        def _():
            remote(
                kv_out.at[0], kv_buf.at[1, 1 - t, b], fwd_s.at[0, s], fwd_r.at[0, s], at(f, h, 1 - t)
            ).wait_recv()

        @pl.when(has_next)
        def _():
            remote(
                kv_out.at[0], kv_buf.at[2, 1 - t, b], fwd_s.at[1, s], fwd_r.at[1, s], at(f, h, 1 - t)
            ).wait_recv()

    group = 2 if Z <= 4 else 1
    masks = (
        jnp.float32(0.0),
        jnp.where(has_prev, 0.0, ABSENT).astype(jnp.float32),
        jnp.where(has_next, 0.0, ABSENT).astype(jnp.float32),
    )
    rate = math.log2(math.e) / math.sqrt(HD)
    keys_all = 2 * Z * T

    def o_send(j):
        return remote(o_out.at[j], o_buf.at[h], o_s.at[j], o_r.at[h], at(f - 1, j, t))

    def lo_send(j):
        return remote(o_out.at[j], lo_buf, o_s.at[j], lo_r, at(h, j, t))

    def attend(i, carry):
        rows = q_buf[pl.ds(i * group, group)].reshape(group * T, HD)
        scores = [
            lax.dot_general(
                rows,
                kv_buf[slot, :, :, 0].reshape(keys_all, HD),
                (((1,), (1,)), ((), ())),
                preferred_element_type=jnp.float32,
            )
            for slot in range(3)
        ]
        highest = jnp.max(scores[0], axis=1, keepdims=True)
        for slot in (1, 2):
            highest = jnp.maximum(highest, jnp.max(scores[slot], axis=1, keepdims=True) - masks[slot])
        total = jnp.zeros((group * T, 1), jnp.float32)
        blended = jnp.zeros((group * T, HD), jnp.float32)
        for slot in range(3):
            weights = jnp.exp2((scores[slot] - (highest + masks[slot])) * rate)
            total = total + jnp.sum(weights, axis=1, keepdims=True)
            blended = blended + jnp.dot(
                weights.astype(jnp.bfloat16),
                kv_buf[slot, :, :, 1].reshape(keys_all, HD),
                preferred_element_type=jnp.float32,
            )
        result = (blended / total).astype(jnp.bfloat16)
        for g in range(group):
            o_out[i * group + g] = result[g * T : (g + 1) * T]
            j = i * group + g

            @pl.when(f > 0)
            def _():
                o_send(j).start()

            @pl.when((f == 0) & ((h != 0) | (j != 0)))
            def _():
                lo_send(j).start()

            @pl.when((f == 0) & (h == 0) & (j == 0))
            def _():
                pltpu.make_async_copy(o_out.at[0], lo_buf, lo_r).start()

        return carry

    lax.fori_loop(0, Z // group, attend, 0)

    @pl.when(f == F - 1)
    def _():
        pltpu.make_async_copy(inc_hbm, nq_ref.at[0], out_sem.at[0]).start()

    @pl.when(f < F - 1)
    def _():
        remote(res_hbm, res_buf, res_s, res_r, at(f, h, 1 - t)).wait_recv()
        remote(gate_out, gate_buf, gate_s, gate_r, at(f, h, 1 - t)).wait_recv()
        for j in range(Z):
            remote(o_out.at[0], o_buf.at[j], o_s.at[0], o_r.at[j], at(f, h, 1 - t)).wait_recv()
            cols = slice(j * HD, (j + 1) * HD)
            nq_buf[:, cols] = (
                res_buf[0, :, cols].astype(jnp.float32) + gate_buf[0:1, cols] * o_buf[j].astype(jnp.float32)
            ).astype(jnp.bfloat16)
        pltpu.make_async_copy(nq_buf, nq_ref.at[0], out_sem.at[0]).start()

    remote(lres_buf, lres_buf, lres_s.at[0], lres_r, at(f, h, 1 - t)).wait_recv()
    remote(lgate_buf, lgate_buf, lgate_s.at[0], lgate_r, at(f, h, 1 - t)).wait_recv()
    remote(lo_buf, lo_buf, o_s.at[0], lo_r, at(f, h, 1 - t)).wait_recv()
    lv_buf[...] = (
        lres_buf[...].astype(jnp.float32) + lgate_buf[0:1, :] * lo_buf[...].astype(jnp.float32)
    ).astype(jnp.bfloat16)
    leave = pltpu.make_async_copy(lv_buf, lv_ref, out_sem.at[1])
    leave.start()

    for s in range(Z):
        if s > 0:
            kv_send(s).wait_send()
            q_send(s).wait_send()
        peer_send(s, 0, kv_out.at[0]).wait_send()

        @pl.when(sends_next)
        def _():
            next_send(s, 0, kv_out.at[0]).wait_send()

        @pl.when(sends_prev)
        def _():
            prev_send(s, 0, kv_out.at[0]).wait_send()

        @pl.when(has_prev)
        def _():
            fwd_send(1, s, 0).wait_send()

        @pl.when(has_next)
        def _():
            fwd_send(2, s, 0).wait_send()

        if relay:

            @pl.when((f == 0) | (f == 3))
            def _():
                relay_down(s, 0).wait_send()

        @pl.when((f > 0) | (h != 0) | (s != 0))
        def _():
            o_send(s).wait_send()

    @pl.when(has_prev)
    def _():
        res_send().wait_send()
        gate_send().wait_send()

    @pl.when(f == 0)
    def _():
        for g in range(1, F):
            lres_send(g).wait_send()
            lgate_send(g).wait_send()

    pltpu.make_async_copy(inc_hbm, nq_ref.at[0], out_sem.at[0]).wait()
    leave.wait()


def solution(mesh):
    F, Z = mesh.shape["frame"], mesh.shape["head"]

    def per_device(queries, keys, values, residual, incoming, gate_table, timesteps, positions):
        T, HH = queries.shape[1], queries.shape[2]
        assert HH == Z * HD and HH == F * HD and mesh.shape["tok"] == 2
        bf, f32 = jnp.bfloat16, jnp.float32
        dma = pltpu.SemaphoreType.DMA
        anywhere = pl.BlockSpec(memory_space=pl.ANY)
        smem = pl.BlockSpec(memory_space=pltpu.SMEM)
        return pl.pallas_call(
            functools.partial(kernel, F, Z, F == 4),
            out_shape=(
                jax.ShapeDtypeStruct((1, T, HH), bf),
                jax.ShapeDtypeStruct((T, HD), bf),
            ),
            in_specs=[anywhere] * 6 + [smem, smem],
            out_specs=(anywhere, anywhere),
            scratch_shapes=[
                pltpu.VMEM((T, HH), bf),
                pltpu.VMEM((T, HH), bf),
                pltpu.VMEM(gate_table.shape, f32),
                pltpu.VMEM((Z, 2, T, HD), bf),
                pltpu.VMEM((Z, T, HD), bf),
                pltpu.VMEM((8, HH), f32),
                pltpu.VMEM((3, 2, Z, 2, T, HD), bf),
                pltpu.VMEM((Z, T, HD), bf),
                pltpu.VMEM((Z, T, HD), bf),
                pltpu.VMEM((Z, T, HD), bf),
                pltpu.VMEM((T, HD), bf),
                pltpu.VMEM((1, T, HH), bf),
                pltpu.VMEM((T, HD), bf),
                pltpu.VMEM((8, HH), f32),
                pltpu.VMEM((8, HD), f32),
                pltpu.VMEM((T, HH), bf),
                pltpu.VMEM((T, HD), bf),
                dma((3,)), dma((Z,)),
                dma((Z,)), dma((Z,)), dma((Z,)), dma((Z,)),
                dma((Z,)), dma((Z,)), dma((2, Z)), dma((2, Z)), dma((Z,)), dma((2, Z)), dma((2, Z)),
                dma((Z,)), dma((Z,)), dma,
                dma, dma, dma((F,)), dma,
                dma, dma, dma((F,)), dma,
                dma((2,)),
            ],
            compiler_params=pltpu.CompilerParams(
                collective_id=0, has_side_effects=True, vmem_limit_bytes=48 * 1024 * 1024
            ),
        )(queries, keys, values, residual, incoming, gate_table, timesteps, positions)

    placed = (
        P("frame", ("head", "tok"), None),
        P("frame", ("head", "tok"), None),
        P("frame", ("head", "tok"), None),
        P("frame", ("head", "tok"), None),
        P(("head", "tok"), None),
        P(),
        P("frame"),
        P("frame"),
    )
    return jax.shard_map(
        per_device,
        mesh=mesh,
        in_specs=placed,
        out_specs=(P("frame", ("head", "tok"), None), P(("head", "tok"), "frame")),
        check_vma=False,
    )
```

```python
import functools
import math

import jax
import jax.numpy as jnp
from jax import lax
from jax.experimental import pallas as pl
from jax.experimental.pallas import tpu as pltpu
from jax.sharding import PartitionSpec as P

HD = 128
HALF = 8
MESH = pl.DeviceIdType.MESH


def kernel(
    frames, heads, relay,
    q_hbm, k_hbm, v_hbm, res_hbm, inc_hbm, gate_hbm, steps_ref, pos_ref,
    nq_ref, lv_ref,
    q_in, k_in, gate_in, kv_out, q_out, gate_out,
    kv_buf, q_buf, o_out, o_buf, lo_buf, res_buf, lres_buf, gate_buf, lgate_buf, nq_buf, lv_buf,
    top, weight_sum, blended_buf,
    load_sem, v_sem, kvz_s, kvz_r, qz_s, qz_r, peer_s, peer_r, fr_s, fr_r, fwd_s, fwd_r,
    o_s, o_r, lo_r, res_s, res_r, lres_s, lres_r, gate_s, gate_r, lgate_s, lgate_r, out_sem,
):
    F, Z = frames, heads
    f = lax.axis_index("frame")
    h = lax.axis_index("head")
    t = lax.axis_index("tok")
    T = q_in.shape[0]
    has_prev = f > 0
    has_across = (f > 0) & (f < F - 1)
    partner = f + 1 - 2 * lax.rem(f, 2)
    across = f - 1 + 2 * lax.rem(f, 2)

    def at(fr, hd, tk):
        return {"frame": fr, "head": hd, "tok": tk}

    def remote(src, dst, send, recv, dev):
        return pltpu.make_async_remote_copy(
            src_ref=src, dst_ref=dst, send_sem=send, recv_sem=recv, device_id=dev, device_id_type=MESH
        )

    load_k = pltpu.make_async_copy(k_hbm.at[0], k_in, load_sem.at[0])
    load_q = pltpu.make_async_copy(q_hbm.at[0], q_in, load_sem.at[1])
    load_gate = pltpu.make_async_copy(gate_hbm, gate_in, load_sem.at[2])
    load_v = [
        pltpu.make_async_copy(v_hbm.at[0, :, pl.ds(j * HD, HD)], kv_out.at[j, 1], v_sem.at[j]) for j in range(Z)
    ]
    load_k.start()
    for c in load_v:
        c.start()
    load_q.start()
    load_gate.start()

    barrier = pltpu.get_barrier_semaphore()
    me = f * Z + h

    def greet(s, carry):
        other = lax.rem(me + s, F * Z)
        pl.semaphore_signal(barrier, inc=1, device_id=at(other // Z, lax.rem(other, Z), t), device_id_type=MESH)
        return carry

    lax.fori_loop(1, F * Z, greet, 0)
    pl.semaphore_signal(barrier, inc=1, device_id=at(f, h, 1 - t), device_id_type=MESH)

    lane = lax.broadcasted_iota(jnp.int32, (8, HD), 1)
    power = lax.rem(lane, HALF).astype(jnp.float32)
    angle = pos_ref[0].astype(jnp.float32) * jnp.exp2(-power)
    cosine = jnp.where(lane < 2 * HALF, jnp.cos(angle), 1.0)[0:1]
    sine = jnp.sin(angle)
    sine_up = jnp.where(lane < HALF, -sine, 0.0)[0:1]
    sine_down = jnp.where((lane >= HALF) & (lane < 2 * HALF), sine, 0.0)[0:1]

    def turned(x):
        x = x.astype(jnp.float32)
        up = pltpu.roll(x, HD - HALF, 1)
        down = pltpu.roll(x, HALF, 1)
        return (x * cosine + up * sine_up + down * sine_down).astype(jnp.bfloat16)

    load_k.wait()
    for j in range(Z):
        kv_out[j, 0] = turned(k_in[:, j * HD : (j + 1) * HD])
    load_q.wait()
    for j in range(Z):
        q_out[j] = turned(q_in[:, j * HD : (j + 1) * HD])
    for c in load_v:
        c.wait()
    pl.semaphore_wait(barrier, F * Z)

    def kv_send(s):
        d = lax.rem(h + s, Z)
        return remote(kv_out.at[d], kv_buf.at[0, t, h], kvz_s.at[s], kvz_r.at[s], at(f, d, t))

    def q_send(s):
        d = lax.rem(h + s, Z)
        return remote(q_out.at[d], q_buf.at[s], qz_s.at[s], qz_r.at[s], at(f, d, t))

    for s in range(1, Z):
        kv_send(s).start()

    def peer_send(s, b, src):
        return remote(src, kv_buf.at[0, t, b], peer_s.at[s], peer_r.at[s], at(f, h, 1 - t))

    def pair_send(s, b, src):
        return remote(src, kv_buf.at[1, t, b], fr_s.at[0, s], fr_r.at[0, s], at(partner, h, t))

    def across_send(s, b, src):
        return remote(src, kv_buf.at[2, t, b], fr_s.at[1, s], fr_r.at[1, s], at(across, h, t))

    def relay_send(s, b):
        return remote(
            kv_buf.at[1, t, b], kv_buf.at[2, t, b], fr_s.at[1, s], fr_r.at[1, s], at(lax.rem(f + 2, F), h, t)
        )

    def fwd_send(slot, s, b):
        ref = kv_buf.at[slot, t, b]
        return remote(ref, ref, fwd_s.at[slot - 1, s], fwd_r.at[slot - 1, s], at(f, h, 1 - t))

    def spread(s, b, src):
        pair_send(s, b, src).start()
        if not relay:

            @pl.when(has_across)
            def _():
                across_send(s, b, src).start()

        peer_send(s, b, src).start()

    spread(0, h, kv_out.at[h])
    for s in range(1, Z):
        q_send(s).start()
    kv_buf[0, t, h] = kv_out[h]
    q_buf[0] = q_out[h]

    load_gate.wait()
    gate_out[...] = jnp.broadcast_to(gate_in[pl.ds(steps_ref[0], 1), :], gate_out.shape)

    def came(ref, sem):
        remote(ref, ref, sem, sem, at(f, h, 1 - t)).wait_recv()

    for s in range(1, Z):
        b = lax.rem(h + Z - s, Z)
        came(kv_buf.at[0, t, b], kvz_r.at[s])
        spread(s, b, kv_buf.at[0, t, b])

    for s in range(Z):
        b = lax.rem(h + Z - s, Z)
        came(kv_buf.at[1, t, b], fr_r.at[0, s])
        if relay:

            @pl.when(jnp.logical_not(has_across))
            def _():
                relay_send(s, b).start()

        fwd_send(1, s, b).start()

    def res_send():
        return remote(res_hbm, res_buf, res_s, res_r, at(f - 1, h, t))

    def gate_send():
        return remote(gate_out, gate_buf, gate_s, gate_r, at(f - 1, h, t))

    def lres_send(g):
        return remote(res_hbm.at[0, :, pl.ds(g * HD, HD)], lres_buf, lres_s.at[g], lres_r, at(g, h, t))

    def lgate_send(g):
        return remote(gate_out.at[:, pl.ds(g * HD, HD)], lgate_buf, lgate_s.at[g], lgate_r, at(g, h, t))

    @pl.when(has_prev)
    def _():
        res_send().start()
        gate_send().start()

    @pl.when(f == 0)
    def _():
        pltpu.make_async_copy(res_hbm.at[0, :, pl.ds(0, HD)], lres_buf, lres_r).start()
        pltpu.make_async_copy(gate_out.at[:, pl.ds(0, HD)], lgate_buf, lgate_r).start()
        for g in range(1, F):
            lres_send(g).start()
            lgate_send(g).start()

    for s in range(Z):
        b = lax.rem(h + s, Z)
        came(kv_buf.at[0, 1 - t, b], peer_r.at[s])

    rate = math.log2(math.e) / math.sqrt(HD)
    keys_all = 2 * Z * T
    group = 2 if Z <= 4 else 1

    def score(rows, slot):
        return lax.dot_general(
            rows,
            kv_buf[slot, :, :, 0].reshape(keys_all, HD),
            (((1,), (1,)), ((), ())),
            preferred_element_type=jnp.float32,
        )

    def blend(weights, slot):
        return jnp.dot(
            weights.astype(jnp.bfloat16),
            kv_buf[slot, :, :, 1].reshape(keys_all, HD),
            preferred_element_type=jnp.float32,
        )

    def near(i, first):
        rows = q_buf[pl.ds(i * group, group)].reshape(group * T, HD)
        own = score(rows, 0)
        if first:
            for s in range(Z):
                b = lax.rem(h + s, Z)
                came(kv_buf.at[1, 1 - t, b], fwd_r.at[0, s])
        beside = score(rows, 1)
        highest = jnp.maximum(jnp.max(own, axis=1, keepdims=True), jnp.max(beside, axis=1, keepdims=True))
        own = jnp.exp2((own - highest) * rate)
        beside = jnp.exp2((beside - highest) * rate)
        at_rows = pl.ds(i * group * T, group * T)
        top[at_rows] = jnp.broadcast_to(highest, (group * T, HD))
        total = jnp.sum(own, axis=1, keepdims=True) + jnp.sum(beside, axis=1, keepdims=True)
        weight_sum[at_rows] = jnp.broadcast_to(total, (group * T, HD))
        blended_buf[at_rows] = blend(own, 0) + blend(beside, 1)

    if Z <= 4:
        for i in range(Z // group):
            for s in range(max(i * group, 1), (i + 1) * group):
                came(q_buf.at[s], qz_r.at[s])
            near(i, i == 0)
    else:
        for s in range(1, Z):
            came(q_buf.at[s], qz_r.at[s])
        near(0, True)
        lax.fori_loop(1, Z // group, lambda i, c: (near(i, False), c)[1], 0)

    @pl.when(has_across)
    def _():
        for s in range(Z):
            b = lax.rem(h + Z - s, Z)
            came(kv_buf.at[2, t, b], fr_r.at[1, s])
            fwd_send(2, s, b).start()
        for s in range(Z):
            b = lax.rem(h + Z - s, Z)
            came(kv_buf.at[2, 1 - t, b], fwd_r.at[1, s])

    def o_send(s):
        return remote(o_out.at[s], o_buf.at[h], o_s.at[s], o_r.at[h], at(f - 1, lax.rem(h + Z - s, Z), t))

    def lo_send(s):
        return remote(o_out.at[s], lo_buf, o_s.at[s], lo_r, at(h, lax.rem(h + Z - s, Z), t))

    def leave_with(result, i):
        for g in range(group):
            s = i * group + g
            o_out[s] = result[g * T : (g + 1) * T]

            @pl.when(f > 0)
            def _():
                o_send(s).start()

            @pl.when((f == 0) & ((h != 0) | (s != 0)))
            def _():
                lo_send(s).start()

            @pl.when((f == 0) & (h == 0) & (s == 0))
            def _():
                pltpu.make_async_copy(o_out.at[0], lo_buf, lo_r).start()

    def finish(i, carry):
        at_rows = pl.ds(i * group * T, group * T)

        @pl.when(has_across)
        def _():
            scores = score(q_buf[pl.ds(i * group, group)].reshape(group * T, HD), 2)
            before = top[at_rows]
            highest = jnp.maximum(before, jnp.max(scores, axis=1, keepdims=True))
            keep = jnp.exp2((before - highest) * rate)
            weights = jnp.exp2((scores - highest[:, 0:1]) * rate)
            total = weight_sum[at_rows] * keep + jnp.sum(weights, axis=1, keepdims=True)
            leave_with(((blended_buf[at_rows] * keep + blend(weights, 2)) / total).astype(jnp.bfloat16), i)

        @pl.when(jnp.logical_not(has_across))
        def _():
            leave_with((blended_buf[at_rows] / weight_sum[at_rows]).astype(jnp.bfloat16), i)

        return carry

    if Z <= 4:
        for i in range(Z // group):
            finish(i, 0)
    else:
        lax.fori_loop(0, Z // group, finish, 0)

    @pl.when(f == F - 1)
    def _():
        pltpu.make_async_copy(inc_hbm, nq_ref.at[0], out_sem.at[0]).start()

    @pl.when(f < F - 1)
    def _():
        remote(res_hbm, res_buf, res_s, res_r, at(f, h, 1 - t)).wait_recv()
        remote(gate_out, gate_buf, gate_s, gate_r, at(f, h, 1 - t)).wait_recv()
        for j in range(Z):
            remote(o_out.at[0], o_buf.at[j], o_s.at[0], o_r.at[j], at(f, h, 1 - t)).wait_recv()
            cols = slice(j * HD, (j + 1) * HD)
            nq_buf[:, cols] = (
                res_buf[0, :, cols].astype(jnp.float32) + gate_buf[0:1, cols] * o_buf[j].astype(jnp.float32)
            ).astype(jnp.bfloat16)
        pltpu.make_async_copy(nq_buf, nq_ref.at[0], out_sem.at[0]).start()

    remote(lres_buf, lres_buf, lres_s.at[0], lres_r, at(f, h, 1 - t)).wait_recv()
    remote(lgate_buf, lgate_buf, lgate_s.at[0], lgate_r, at(f, h, 1 - t)).wait_recv()
    remote(lo_buf, lo_buf, o_s.at[0], lo_r, at(f, h, 1 - t)).wait_recv()
    lv_buf[...] = (
        lres_buf[...].astype(jnp.float32) + lgate_buf[0:1, :] * lo_buf[...].astype(jnp.float32)
    ).astype(jnp.bfloat16)
    leave = pltpu.make_async_copy(lv_buf, lv_ref, out_sem.at[1])
    leave.start()

    for s in range(Z):
        if s > 0:
            kv_send(s).wait_send()
            q_send(s).wait_send()
        peer_send(s, 0, kv_out.at[0]).wait_send()
        pair_send(s, 0, kv_out.at[0]).wait_send()
        fwd_send(1, s, 0).wait_send()

        @pl.when(has_across)
        def _():
            fwd_send(2, s, 0).wait_send()

        if relay:

            @pl.when(jnp.logical_not(has_across))
            def _():
                relay_send(s, 0).wait_send()

        else:

            @pl.when(has_across)
            def _():
                across_send(s, 0, kv_out.at[0]).wait_send()

        @pl.when((f > 0) | (h != 0) | (s != 0))
        def _():
            o_send(s).wait_send()

    @pl.when(has_prev)
    def _():
        res_send().wait_send()
        gate_send().wait_send()

    @pl.when(f == 0)
    def _():
        for g in range(1, F):
            lres_send(g).wait_send()
            lgate_send(g).wait_send()

    pltpu.make_async_copy(inc_hbm, nq_ref.at[0], out_sem.at[0]).wait()
    leave.wait()


def solution(mesh):
    F, Z = mesh.shape["frame"], mesh.shape["head"]

    def per_device(queries, keys, values, residual, incoming, gate_table, timesteps, positions):
        T, HH = queries.shape[1], queries.shape[2]
        assert HH == Z * HD and HH == F * HD and mesh.shape["tok"] == 2
        bf, f32 = jnp.bfloat16, jnp.float32
        dma = pltpu.SemaphoreType.DMA
        anywhere = pl.BlockSpec(memory_space=pl.ANY)
        smem = pl.BlockSpec(memory_space=pltpu.SMEM)
        return pl.pallas_call(
            functools.partial(kernel, F, Z, F == 4),
            out_shape=(
                jax.ShapeDtypeStruct((1, T, HH), bf),
                jax.ShapeDtypeStruct((T, HD), bf),
            ),
            in_specs=[anywhere] * 6 + [smem, smem],
            out_specs=(anywhere, anywhere),
            scratch_shapes=[
                pltpu.VMEM((T, HH), bf),
                pltpu.VMEM((T, HH), bf),
                pltpu.VMEM(gate_table.shape, f32),
                pltpu.VMEM((Z, 2, T, HD), bf),
                pltpu.VMEM((Z, T, HD), bf),
                pltpu.VMEM((8, HH), f32),
                pltpu.VMEM((3, 2, Z, 2, T, HD), bf),
                pltpu.VMEM((Z, T, HD), bf),
                pltpu.VMEM((Z, T, HD), bf),
                pltpu.VMEM((Z, T, HD), bf),
                pltpu.VMEM((T, HD), bf),
                pltpu.VMEM((1, T, HH), bf),
                pltpu.VMEM((T, HD), bf),
                pltpu.VMEM((8, HH), f32),
                pltpu.VMEM((8, HD), f32),
                pltpu.VMEM((T, HH), bf),
                pltpu.VMEM((T, HD), bf),
                pltpu.VMEM((Z * T, HD), f32),
                pltpu.VMEM((Z * T, HD), f32),
                pltpu.VMEM((Z * T, HD), f32),
                dma((3,)), dma((Z,)),
                dma((Z,)), dma((Z,)), dma((Z,)), dma((Z,)),
                dma((Z,)), dma((Z,)), dma((2, Z)), dma((2, Z)), dma((2, Z)), dma((2, Z)),
                dma((Z,)), dma((Z,)), dma,
                dma, dma, dma((F,)), dma,
                dma, dma, dma((F,)), dma,
                dma((2,)),
            ],
            compiler_params=pltpu.CompilerParams(
                collective_id=0, has_side_effects=True, vmem_limit_bytes=60 * 1024 * 1024
            ),
        )(queries, keys, values, residual, incoming, gate_table, timesteps, positions)

    placed = (
        P("frame", ("head", "tok"), None),
        P("frame", ("head", "tok"), None),
        P("frame", ("head", "tok"), None),
        P("frame", ("head", "tok"), None),
        P(("head", "tok"), None),
        P(),
        P("frame"),
        P("frame"),
    )
    return jax.shard_map(
        per_device,
        mesh=mesh,
        in_specs=placed,
        out_specs=(P("frame", ("head", "tok"), None), P(("head", "tok"), "frame")),
        check_vma=False,
    )
```

```python
import functools
import math

import jax
import jax.numpy as jnp
from jax import lax
from jax.experimental import pallas as pl
from jax.experimental.pallas import tpu as pltpu
from jax.sharding import PartitionSpec as P

HD = 128
HALF = 8
MESH = pl.DeviceIdType.MESH


def kernel(
    frames, heads, relay,
    q_hbm, k_hbm, v_hbm, res_hbm, inc_hbm, gate_hbm, steps_ref, pos_ref,
    nq_ref, lv_ref,
    q_in, k_in, gate_in, kv_out, q_out, gate_out,
    kv_buf, q_buf, o_out, o_buf, lo_buf, res_buf, lres_buf, gate_buf, lgate_buf,
    top, weight_sum, blended_buf,
    load_sem, v_sem, kvz_s, kvz_r, qz_s, qz_r, peer_s, peer_r, fr_s, fr_r, fwd_s, fwd_r,
    o_s, o_r, lo_r, res_s, res_r, lres_s, lres_r, gate_s, gate_r, lgate_s, lgate_r, out_sem,
):
    F, Z = frames, heads
    f = lax.axis_index("frame")
    h = lax.axis_index("head")
    t = lax.axis_index("tok")
    T = q_in.shape[0]
    has_prev = f > 0
    has_across = (f > 0) & (f < F - 1)
    partner = f + 1 - 2 * lax.rem(f, 2)
    across = f - 1 + 2 * lax.rem(f, 2)

    def at(fr, hd, tk):
        return {"frame": fr, "head": hd, "tok": tk}

    def remote(src, dst, send, recv, dev):
        return pltpu.make_async_remote_copy(
            src_ref=src, dst_ref=dst, send_sem=send, recv_sem=recv, device_id=dev, device_id_type=MESH
        )

    load_k = pltpu.make_async_copy(k_hbm.at[0], k_in, load_sem.at[0])
    load_q = pltpu.make_async_copy(q_hbm.at[0], q_in, load_sem.at[1])
    load_gate = pltpu.make_async_copy(gate_hbm, gate_in, load_sem.at[2])
    load_v = [
        pltpu.make_async_copy(v_hbm.at[0, :, pl.ds(j * HD, HD)], kv_out.at[j, 1], v_sem.at[j]) for j in range(Z)
    ]
    incoming = pltpu.make_async_copy(inc_hbm, nq_ref.at[0], out_sem)
    load_q.start()
    load_k.start()
    for c in load_v:
        c.start()
    load_gate.start()

    @pl.when(f == F - 1)
    def _():
        incoming.start()

    barrier = pltpu.get_barrier_semaphore()
    me = f * Z + h

    def greet(s, carry):
        other = lax.rem(me + s, F * Z)
        pl.semaphore_signal(barrier, inc=1, device_id=at(other // Z, lax.rem(other, Z), t), device_id_type=MESH)
        return carry

    lax.fori_loop(1, F * Z, greet, 0)
    pl.semaphore_signal(barrier, inc=1, device_id=at(f, h, 1 - t), device_id_type=MESH)

    lane = lax.broadcasted_iota(jnp.int32, (8, HD), 1)
    power = lax.rem(lane, HALF).astype(jnp.float32)
    angle = pos_ref[0].astype(jnp.float32) * jnp.exp2(-power)
    cosine = jnp.where(lane < 2 * HALF, jnp.cos(angle), 1.0)[0:1]
    sine = jnp.sin(angle)
    sine_up = jnp.where(lane < HALF, -sine, 0.0)[0:1]
    sine_down = jnp.where((lane >= HALF) & (lane < 2 * HALF), sine, 0.0)[0:1]

    def turned(x):
        x = x.astype(jnp.float32)
        up = pltpu.roll(x, HD - HALF, 1)
        down = pltpu.roll(x, HALF, 1)
        return (x * cosine + up * sine_up + down * sine_down).astype(jnp.bfloat16)

    load_q.wait()
    for j in range(Z):
        q_out[j] = turned(q_in[:, j * HD : (j + 1) * HD])
    load_k.wait()
    for j in range(Z):
        kv_out[j, 0] = turned(k_in[:, j * HD : (j + 1) * HD])
    for c in load_v:
        c.wait()
    pl.semaphore_wait(barrier, F * Z)

    def q_send(s):
        return remote(q_out.at[lax.rem(h + s, Z)], q_buf.at[s], qz_s.at[s], qz_r.at[s], at(f, lax.rem(h + s, Z), t))

    def kv_send(s):
        d = lax.rem(h + s, Z)
        return remote(kv_out.at[d], kv_buf.at[0, s, t], kvz_s.at[s], kvz_r.at[s], at(f, d, t))

    for s in range(1, Z):
        q_send(s).start()
    for s in range(1, Z):
        kv_send(s).start()

    def peer_send(s, src):
        return remote(src, kv_buf.at[0, s, t], peer_s.at[s], peer_r.at[s], at(f, h, 1 - t))

    def pair_send(s, src):
        return remote(src, kv_buf.at[1, s, t], fr_s.at[0, s], fr_r.at[0, s], at(partner, h, t))

    def across_send(s, src):
        return remote(src, kv_buf.at[2, s, t], fr_s.at[1, s], fr_r.at[1, s], at(across, h, t))

    def relay_send(s):
        return remote(
            kv_buf.at[1, s, t], kv_buf.at[2, s, t], fr_s.at[1, s], fr_r.at[1, s], at(lax.rem(f + 2, F), h, t)
        )

    def fwd_send(slot, s):
        ref = kv_buf.at[slot, s, t]
        return remote(ref, ref, fwd_s.at[slot - 1, s], fwd_r.at[slot - 1, s], at(f, h, 1 - t))

    def spread(s, src):
        pair_send(s, src).start()
        if not relay:

            @pl.when(has_across)
            def _():
                across_send(s, src).start()

        peer_send(s, src).start()

    spread(0, kv_out.at[h])
    kv_buf[0, 0, t] = kv_out[h]
    q_buf[0] = q_out[h]

    load_gate.wait()
    gate_out[...] = jnp.broadcast_to(gate_in[pl.ds(steps_ref[0], 1), :], gate_out.shape)

    def came(ref, sem):
        remote(ref, ref, sem, sem, at(f, h, 1 - t)).wait_recv()

    def take_own(s):
        came(kv_buf.at[0, s, t], kvz_r.at[s])
        spread(s, kv_buf.at[0, s, t])

    def take_pair(s):
        came(kv_buf.at[1, s, t], fr_r.at[0, s])
        if relay:

            @pl.when(jnp.logical_not(has_across))
            def _():
                relay_send(s).start()

        fwd_send(1, s).start()

    def take_across(s):
        @pl.when(has_across)
        def _():
            came(kv_buf.at[2, s, t], fr_r.at[1, s])
            fwd_send(2, s).start()

    def res_send():
        return remote(res_hbm, res_buf, res_s, res_r, at(f - 1, h, t))

    def gate_send():
        return remote(gate_out, gate_buf, gate_s, gate_r, at(f - 1, h, t))

    def lres_send(g):
        return remote(res_hbm.at[0, :, pl.ds(g * HD, HD)], lres_buf, lres_s.at[g], lres_r, at(g, h, t))

    def lgate_send(g):
        return remote(gate_out.at[:, pl.ds(g * HD, HD)], lgate_buf, lgate_s.at[g], lgate_r, at(g, h, t))

    def send_residual():
        @pl.when(has_prev)
        def _():
            res_send().start()
            gate_send().start()

        @pl.when(f == 0)
        def _():
            pltpu.make_async_copy(res_hbm.at[0, :, pl.ds(0, HD)], lres_buf, lres_r).start()
            pltpu.make_async_copy(gate_out.at[:, pl.ds(0, HD)], lgate_buf, lgate_r).start()
            for g in range(1, F):
                lres_send(g).start()
                lgate_send(g).start()

    rate = math.log2(math.e) / math.sqrt(HD)

    def merged(i, blocks, parts, first):
        rows = q_buf[pl.ds(i, blocks)].reshape(blocks * T, HD)
        at_rows = pl.ds(i * T, blocks * T)
        near_keys = jnp.concatenate([kv_buf[p, s, :, 0].reshape(2 * T, HD) for p, s in parts])
        near_values = jnp.concatenate([kv_buf[p, s, :, 1].reshape(2 * T, HD) for p, s in parts])
        scores = lax.dot_general(rows, near_keys, (((1,), (1,)), ((), ())), preferred_element_type=jnp.float32)
        highest = jnp.max(scores, axis=1, keepdims=True)
        if not first:
            before = top[at_rows]
            highest = jnp.maximum(before, highest)
            keep = jnp.exp2((before - highest) * rate)
        weights = jnp.exp2((scores - highest[:, 0:1]) * rate)
        total = jnp.sum(weights, axis=1, keepdims=True)
        blended = jnp.dot(weights.astype(jnp.bfloat16), near_values, preferred_element_type=jnp.float32)
        if not first:
            total = weight_sum[at_rows] * keep + total
            blended = blended_buf[at_rows] * keep + blended
        return highest, total, blended

    def gather(parts, first):
        blocks = min(Z, 4)

        def step(i, carry):
            highest, total, blended = merged(i * blocks, blocks, parts, first)
            at_rows = pl.ds(i * blocks * T, blocks * T)
            top[at_rows] = jnp.broadcast_to(highest, (blocks * T, HD))
            weight_sum[at_rows] = jnp.broadcast_to(total, (blocks * T, HD))
            blended_buf[at_rows] = blended
            return carry

        if Z == blocks:
            step(0, 0)
        else:
            lax.fori_loop(0, Z // blocks, step, 0)

    def near(s):
        came(kv_buf.at[0, s, 1 - t], peer_r.at[s])
        came(kv_buf.at[1, s, 1 - t], fwd_r.at[0, s])
        gather([(0, s), (1, s)], s == 0)

    def wait_across(s):
        for p in (s, s + 1):
            came(kv_buf.at[2, p, 1 - t], fwd_r.at[1, p])

    def far(s):
        @pl.when(has_across)
        def _():
            wait_across(s)
            gather([(2, s), (2, s + 1)], False)

    for s in range(Z):
        if s + 1 < Z:
            take_own(s + 1)
        take_pair(s)
        if s == Z - 1:
            send_residual()
        if s == 1:
            for p in range(1, Z):
                came(q_buf.at[p], qz_r.at[p])
        if s >= 1:
            near(s - 1)
        if s >= 2:
            take_across(s - 2)
        if s >= 3 and s % 2 == 1:
            far(s - 3)
    take_across(Z - 2)
    near(Z - 1)

    def o_send(s):
        return remote(o_out.at[s], o_buf.at[h], o_s.at[s], o_r.at[h], at(f - 1, lax.rem(h + Z - s, Z), t))

    def lo_send(s):
        return remote(o_out.at[s], lo_buf, o_s.at[s], lo_r, at(h, lax.rem(h + Z - s, Z), t))

    group = 2

    def leave_with(blended, total, i):
        result = (blended / total).astype(jnp.bfloat16)
        for g in range(group):
            s = i * group + g
            o_out[s] = result[g * T : (g + 1) * T]

            @pl.when(f > 0)
            def _():
                o_send(s).start()

            @pl.when((f == 0) & ((h != 0) | (s != 0)))
            def _():
                lo_send(s).start()

            @pl.when((f == 0) & (h == 0) & (s == 0))
            def _():
                pltpu.make_async_copy(o_out.at[0], lo_buf, lo_r).start()

    def each_group(body):
        if Z <= 4:
            for i in range(Z // group):
                body(i, 0)
        else:
            lax.fori_loop(0, Z // group, body, 0)

    @pl.when(has_across)
    def _():
        came(kv_buf.at[2, Z - 1, t], fr_r.at[1, Z - 1])
        fwd_send(2, Z - 1).start()
        wait_across(Z - 2)

        def last(i, carry):
            _, total, blended = merged(i * group, group, [(2, Z - 2), (2, Z - 1)], False)
            leave_with(blended, total, i)
            return carry

        each_group(last)

    @pl.when(jnp.logical_not(has_across))
    def _():
        def last(i, carry):
            at_rows = pl.ds(i * group * T, group * T)
            leave_with(blended_buf[at_rows], weight_sum[at_rows], i)
            return carry

        each_group(last)

    came(lres_buf, lres_r)
    came(lgate_buf, lgate_r)
    came(lo_buf, lo_r)
    lv_ref[...] = (
        lres_buf[...].astype(jnp.float32) + lgate_buf[0:1, :] * lo_buf[...].astype(jnp.float32)
    ).astype(jnp.bfloat16)

    @pl.when(f < F - 1)
    def _():
        came(res_buf, res_r)
        came(gate_buf, gate_r)
        for j in range(Z):
            came(o_buf.at[j], o_r.at[j])
            cols = slice(j * HD, (j + 1) * HD)
            nq_ref[0, :, cols] = (
                res_buf[0, :, cols].astype(jnp.float32) + gate_buf[0:1, cols] * o_buf[j].astype(jnp.float32)
            ).astype(jnp.bfloat16)

    @pl.when(f == F - 1)
    def _():
        incoming.wait()

    for s in range(Z):
        if s > 0:
            kv_send(s).wait_send()
            q_send(s).wait_send()
        peer_send(s, kv_out.at[0]).wait_send()
        pair_send(s, kv_out.at[0]).wait_send()
        fwd_send(1, s).wait_send()

        @pl.when(has_across)
        def _():
            fwd_send(2, s).wait_send()

        if relay:

            @pl.when(jnp.logical_not(has_across))
            def _():
                relay_send(s).wait_send()

        else:

            @pl.when(has_across)
            def _():
                across_send(s, kv_out.at[0]).wait_send()

        @pl.when((f > 0) | (h != 0) | (s != 0))
        def _():
            o_send(s).wait_send()

    @pl.when(has_prev)
    def _():
        res_send().wait_send()
        gate_send().wait_send()

    @pl.when(f == 0)
    def _():
        for g in range(1, F):
            lres_send(g).wait_send()
            lgate_send(g).wait_send()


def solution(mesh):
    F, Z = mesh.shape["frame"], mesh.shape["head"]

    def per_device(queries, keys, values, residual, incoming, gate_table, timesteps, positions):
        T, HH = queries.shape[1], queries.shape[2]
        assert HH == Z * HD and HH == F * HD and mesh.shape["tok"] == 2
        blocks = (queries, keys, values, residual, incoming, gate_table)
        bf, f32 = jnp.bfloat16, jnp.float32
        dma = pltpu.SemaphoreType.DMA
        anywhere = pl.BlockSpec(memory_space=pl.ANY)
        smem = pl.BlockSpec(memory_space=pltpu.SMEM)
        return pl.pallas_call(
            functools.partial(kernel, F, Z, F == 4),
            out_shape=(
                jax.ShapeDtypeStruct((1, T, HH), bf),
                jax.ShapeDtypeStruct((T, HD), bf),
            ),
            in_specs=[anywhere] * 6 + [smem, smem],
            out_specs=(pl.BlockSpec(memory_space=pltpu.VMEM),) * 2,
            scratch_shapes=[
                pltpu.VMEM((T, HH), bf),
                pltpu.VMEM((T, HH), bf),
                pltpu.VMEM(gate_table.shape, f32),
                pltpu.VMEM((Z, 2, T, HD), bf),
                pltpu.VMEM((Z, T, HD), bf),
                pltpu.VMEM((8, HH), f32),
                pltpu.VMEM((3, Z, 2, 2, T, HD), bf),
                pltpu.VMEM((Z, T, HD), bf),
                pltpu.VMEM((Z, T, HD), bf),
                pltpu.VMEM((Z, T, HD), bf),
                pltpu.VMEM((T, HD), bf),
                pltpu.VMEM((1, T, HH), bf),
                pltpu.VMEM((T, HD), bf),
                pltpu.VMEM((8, HH), f32),
                pltpu.VMEM((8, HD), f32),
                pltpu.VMEM((Z * T, HD), f32),
                pltpu.VMEM((Z * T, HD), f32),
                pltpu.VMEM((Z * T, HD), f32),
                dma((3,)), dma((Z,)),
                dma((Z,)), dma((Z,)), dma((Z,)), dma((Z,)),
                dma((Z,)), dma((Z,)), dma((2, Z)), dma((2, Z)), dma((2, Z)), dma((2, Z)),
                dma((Z,)), dma((Z,)), dma,
                dma, dma, dma((F,)), dma,
                dma, dma, dma((F,)), dma,
                dma,
            ],
            compiler_params=pltpu.CompilerParams(
                collective_id=0, has_side_effects=True, vmem_limit_bytes=48 * 1024 * 1024
            ),
        )(
            *(pltpu.with_memory_space_constraint(x, pltpu.HBM) for x in blocks), timesteps, positions
        )

    placed = (
        P("frame", ("head", "tok"), None),
        P("frame", ("head", "tok"), None),
        P("frame", ("head", "tok"), None),
        P("frame", ("head", "tok"), None),
        P(("head", "tok"), None),
        P(),
        P("frame"),
        P("frame"),
    )
    return jax.shard_map(
        per_device,
        mesh=mesh,
        in_specs=placed,
        out_specs=(P("frame", ("head", "tok"), None), P(("head", "tok"), "frame")),
        check_vma=False,
    )
```

```python
import functools
import math

import jax
import jax.numpy as jnp
from jax import lax
from jax.experimental import pallas as pl
from jax.experimental.pallas import tpu as pltpu
from jax.sharding import PartitionSpec as P

HD = 128
HALF = 8
MESH = pl.DeviceIdType.MESH


def kernel(
    frames, heads, relay,
    q_hbm, k_hbm, v_hbm, res_hbm, inc_hbm, gate_hbm, steps_ref, pos_ref,
    nq_ref, lv_ref,
    q_in, k_in, gate_in, kv_out, q_out, gate_out,
    kv_buf, q_buf, o_out, o_buf, lo_buf, res_buf, lres_buf, gate_buf, lgate_buf,
    q_cols, top, weight_sum, blended_buf,
    load_sem, v_sem, kvz_s, kvz_r, qz_s, qz_r, peer_s, peer_r, fr_s, fr_r, fwd_s, fwd_r,
    o_s, o_r, lo_r, res_s, res_r, lres_s, lres_r, gate_s, gate_r, lgate_s, lgate_r, out_sem,
):
    F, Z = frames, heads
    f = lax.axis_index("frame")
    h = lax.axis_index("head")
    t = lax.axis_index("tok")
    T = q_in.shape[0]
    has_prev = f > 0
    has_across = (f > 0) & (f < F - 1)
    partner = f + 1 - 2 * lax.rem(f, 2)
    across = f - 1 + 2 * lax.rem(f, 2)

    def at(fr, hd, tk):
        return {"frame": fr, "head": hd, "tok": tk}

    def remote(src, dst, send, recv, dev):
        return pltpu.make_async_remote_copy(
            src_ref=src, dst_ref=dst, send_sem=send, recv_sem=recv, device_id=dev, device_id_type=MESH
        )

    load_k = pltpu.make_async_copy(k_hbm.at[0], k_in, load_sem.at[0])
    load_q = pltpu.make_async_copy(q_hbm.at[0], q_in, load_sem.at[1])
    load_gate = pltpu.make_async_copy(gate_hbm, gate_in, load_sem.at[2])
    load_v = [
        pltpu.make_async_copy(v_hbm.at[0, :, pl.ds(j * HD, HD)], kv_out.at[j, 1], v_sem.at[j]) for j in range(Z)
    ]
    incoming = pltpu.make_async_copy(inc_hbm, nq_ref.at[0], out_sem)
    load_q.start()
    load_k.start()
    for c in load_v:
        c.start()
    load_gate.start()

    @pl.when(f == F - 1)
    def _():
        incoming.start()

    barrier = pltpu.get_barrier_semaphore()
    me = f * Z + h

    def greet(s, carry):
        other = lax.rem(me + s, F * Z)
        pl.semaphore_signal(barrier, inc=1, device_id=at(other // Z, lax.rem(other, Z), t), device_id_type=MESH)
        return carry

    lax.fori_loop(1, F * Z, greet, 0)
    pl.semaphore_signal(barrier, inc=1, device_id=at(f, h, 1 - t), device_id_type=MESH)

    lane = lax.broadcasted_iota(jnp.int32, (8, HD), 1)
    power = lax.rem(lane, HALF).astype(jnp.float32)
    angle = pos_ref[0].astype(jnp.float32) * jnp.exp2(-power)
    cosine = jnp.where(lane < 2 * HALF, jnp.cos(angle), 1.0)[0:1]
    sine = jnp.sin(angle)
    sine_up = jnp.where(lane < HALF, -sine, 0.0)[0:1]
    sine_down = jnp.where((lane >= HALF) & (lane < 2 * HALF), sine, 0.0)[0:1]

    def turned(x):
        x = x.astype(jnp.float32)
        up = pltpu.roll(x, HD - HALF, 1)
        down = pltpu.roll(x, HALF, 1)
        return (x * cosine + up * sine_up + down * sine_down).astype(jnp.bfloat16)

    load_q.wait()
    for j in range(Z):
        q_out[j] = turned(q_in[:, j * HD : (j + 1) * HD])
    load_k.wait()
    for j in range(Z):
        kv_out[j, 0] = turned(k_in[:, j * HD : (j + 1) * HD])
    for c in load_v:
        c.wait()
    pl.semaphore_wait(barrier, F * Z)

    def q_send(s):
        return remote(q_out.at[lax.rem(h + s, Z)], q_buf.at[s], qz_s.at[s], qz_r.at[s], at(f, lax.rem(h + s, Z), t))

    def kv_send(s):
        d = lax.rem(h + s, Z)
        return remote(kv_out.at[d], kv_buf.at[0, s, t], kvz_s.at[s], kvz_r.at[s], at(f, d, t))

    for s in range(1, Z):
        q_send(s).start()
    for s in range(1, Z):
        kv_send(s).start()

    def peer_send(s, src):
        return remote(src, kv_buf.at[0, s, t], peer_s.at[s], peer_r.at[s], at(f, h, 1 - t))

    def pair_send(s, src):
        return remote(src, kv_buf.at[1, s, t], fr_s.at[0, s], fr_r.at[0, s], at(partner, h, t))

    def across_send(s, src):
        return remote(src, kv_buf.at[2, s, t], fr_s.at[1, s], fr_r.at[1, s], at(across, h, t))

    def relay_send(s):
        return remote(
            kv_buf.at[1, s, t], kv_buf.at[2, s, t], fr_s.at[1, s], fr_r.at[1, s], at(lax.rem(f + 2, F), h, t)
        )

    def fwd_send(slot, s):
        ref = kv_buf.at[slot, s, t]
        return remote(ref, ref, fwd_s.at[slot - 1, s], fwd_r.at[slot - 1, s], at(f, h, 1 - t))

    def spread(s, src):
        pair_send(s, src).start()
        if not relay:

            @pl.when(has_across)
            def _():
                across_send(s, src).start()

        peer_send(s, src).start()

    spread(0, kv_out.at[h])
    kv_buf[0, 0, t] = kv_out[h]
    q_buf[0] = q_out[h]

    load_gate.wait()
    gate_out[...] = jnp.broadcast_to(gate_in[pl.ds(steps_ref[0], 1), :], gate_out.shape)

    def came(ref, sem):
        remote(ref, ref, sem, sem, at(f, h, 1 - t)).wait_recv()

    def take_own(s):
        came(kv_buf.at[0, s, t], kvz_r.at[s])
        spread(s, kv_buf.at[0, s, t])

    def take_pair(s):
        came(kv_buf.at[1, s, t], fr_r.at[0, s])
        if relay:

            @pl.when(jnp.logical_not(has_across))
            def _():
                relay_send(s).start()

        fwd_send(1, s).start()

    def take_across(s):
        @pl.when(has_across)
        def _():
            came(kv_buf.at[2, s, t], fr_r.at[1, s])
            fwd_send(2, s).start()

    def res_send():
        return remote(res_hbm, res_buf, res_s, res_r, at(f - 1, h, t))

    def gate_send():
        return remote(gate_out, gate_buf, gate_s, gate_r, at(f - 1, h, t))

    def lres_send(g):
        return remote(res_hbm.at[0, :, pl.ds(g * HD, HD)], lres_buf, lres_s.at[g], lres_r, at(g, h, t))

    def lgate_send(g):
        return remote(gate_out.at[:, pl.ds(g * HD, HD)], lgate_buf, lgate_s.at[g], lgate_r, at(g, h, t))

    def send_residual():
        @pl.when(has_prev)
        def _():
            res_send().start()
            gate_send().start()

        @pl.when(f == 0)
        def _():
            pltpu.make_async_copy(res_hbm.at[0, :, pl.ds(0, HD)], lres_buf, lres_r).start()
            pltpu.make_async_copy(gate_out.at[:, pl.ds(0, HD)], lgate_buf, lgate_r).start()
            for g in range(1, F):
                lres_send(g).start()
                lgate_send(g).start()

    rate = math.log2(math.e) / math.sqrt(HD)
    group = min(Z, 4)
    width = group * T

    def columns(i):
        return pl.ds(i * width, width)

    def turn_queries(i, carry):
        rows = q_buf[pl.ds(i * group, group)].reshape(width, HD)
        q_cols[:, columns(i)] = rows.T
        return carry

    def merged(i, keys, values, first):
        scores = jnp.dot(keys, q_cols[:, columns(i)], preferred_element_type=jnp.float32)
        highest = jnp.max(scores, axis=0, keepdims=True)
        if not first:
            before = top[0:1, columns(i)]
            highest = jnp.maximum(before, highest)
            keep = jnp.exp2((before - highest) * rate)
        weights = jnp.exp2((scores - highest) * rate)
        total = jnp.sum(weights, axis=0, keepdims=True)
        blended = jnp.dot(values, weights.astype(jnp.bfloat16), preferred_element_type=jnp.float32)
        if not first:
            total = weight_sum[0:1, columns(i)] * keep + total
            blended = blended_buf[:, columns(i)] * keep + blended
        return highest, total, blended

    def block_pair(parts):
        keys = jnp.concatenate([kv_buf[p, s, :, 0].reshape(2 * T, HD) for p, s in parts])
        values = jnp.concatenate([kv_buf[p, s, :, 1].reshape(2 * T, HD) for p, s in parts])
        return keys, values.T

    def each_group(body):
        if Z == group:
            body(0, 0)
        else:
            lax.fori_loop(0, Z // group, body, 0)

    def gather(parts, first):
        keys, values = block_pair(parts)

        def step(i, carry):
            highest, total, blended = merged(i, keys, values, first)
            top[0:1, columns(i)] = highest
            weight_sum[0:1, columns(i)] = total
            blended_buf[:, columns(i)] = blended
            return carry

        each_group(step)

    def near(s):
        came(kv_buf.at[0, s, 1 - t], peer_r.at[s])
        came(kv_buf.at[1, s, 1 - t], fwd_r.at[0, s])
        gather([(0, s), (1, s)], s == 0)

    def wait_across(s):
        for p in (s, s + 1):
            came(kv_buf.at[2, p, 1 - t], fwd_r.at[1, p])

    def far(s):
        @pl.when(has_across)
        def _():
            wait_across(s)
            gather([(2, s), (2, s + 1)], False)

    for s in range(Z):
        if s + 1 < Z:
            take_own(s + 1)
        take_pair(s)
        if s == Z - 1:
            send_residual()
        if s == 1:
            for p in range(1, Z):
                came(q_buf.at[p], qz_r.at[p])
            each_group(turn_queries)
        if s >= 1:
            near(s - 1)
        if s >= 2:
            take_across(s - 2)
        if s >= 3 and s % 2 == 1:
            far(s - 3)
    take_across(Z - 2)
    near(Z - 1)

    def o_send(s):
        return remote(o_out.at[s], o_buf.at[h], o_s.at[s], o_r.at[h], at(f - 1, lax.rem(h + Z - s, Z), t))

    def lo_send(s):
        return remote(o_out.at[s], lo_buf, o_s.at[s], lo_r, at(h, lax.rem(h + Z - s, Z), t))

    def leave_with(blended, total, i):
        result = (blended / total).T.astype(jnp.bfloat16)
        for g in range(group):
            s = i * group + g
            o_out[s] = result[g * T : (g + 1) * T]

            @pl.when(f > 0)
            def _():
                o_send(s).start()

            @pl.when((f == 0) & ((h != 0) | (s != 0)))
            def _():
                lo_send(s).start()

            @pl.when((f == 0) & (h == 0) & (s == 0))
            def _():
                pltpu.make_async_copy(o_out.at[0], lo_buf, lo_r).start()

    @pl.when(has_across)
    def _():
        came(kv_buf.at[2, Z - 1, t], fr_r.at[1, Z - 1])
        fwd_send(2, Z - 1).start()
        wait_across(Z - 2)
        keys, values = block_pair([(2, Z - 2), (2, Z - 1)])

        def last(i, carry):
            _, total, blended = merged(i, keys, values, False)
            leave_with(blended, total, i)
            return carry

        each_group(last)

    @pl.when(jnp.logical_not(has_across))
    def _():
        def last(i, carry):
            leave_with(blended_buf[:, columns(i)], weight_sum[0:1, columns(i)], i)
            return carry

        each_group(last)

    came(lres_buf, lres_r)
    came(lgate_buf, lgate_r)
    came(lo_buf, lo_r)
    lv_ref[...] = (
        lres_buf[...].astype(jnp.float32) + lgate_buf[0:1, :] * lo_buf[...].astype(jnp.float32)
    ).astype(jnp.bfloat16)

    @pl.when(f < F - 1)
    def _():
        came(res_buf, res_r)
        came(gate_buf, gate_r)
        for j in range(Z):
            came(o_buf.at[j], o_r.at[j])
            cols = slice(j * HD, (j + 1) * HD)
            nq_ref[0, :, cols] = (
                res_buf[0, :, cols].astype(jnp.float32) + gate_buf[0:1, cols] * o_buf[j].astype(jnp.float32)
            ).astype(jnp.bfloat16)

    @pl.when(f == F - 1)
    def _():
        incoming.wait()

    for s in range(Z):
        if s > 0:
            kv_send(s).wait_send()
            q_send(s).wait_send()
        peer_send(s, kv_out.at[0]).wait_send()
        pair_send(s, kv_out.at[0]).wait_send()
        fwd_send(1, s).wait_send()

        @pl.when(has_across)
        def _():
            fwd_send(2, s).wait_send()

        if relay:

            @pl.when(jnp.logical_not(has_across))
            def _():
                relay_send(s).wait_send()

        else:

            @pl.when(has_across)
            def _():
                across_send(s, kv_out.at[0]).wait_send()

        @pl.when((f > 0) | (h != 0) | (s != 0))
        def _():
            o_send(s).wait_send()

    @pl.when(has_prev)
    def _():
        res_send().wait_send()
        gate_send().wait_send()

    @pl.when(f == 0)
    def _():
        for g in range(1, F):
            lres_send(g).wait_send()
            lgate_send(g).wait_send()


def solution(mesh):
    F, Z = mesh.shape["frame"], mesh.shape["head"]

    def per_device(queries, keys, values, residual, incoming, gate_table, timesteps, positions):
        T, HH = queries.shape[1], queries.shape[2]
        assert HH == Z * HD and HH == F * HD and mesh.shape["tok"] == 2
        blocks = (queries, keys, values, residual, incoming, gate_table)
        bf, f32 = jnp.bfloat16, jnp.float32
        dma = pltpu.SemaphoreType.DMA
        anywhere = pl.BlockSpec(memory_space=pl.ANY)
        smem = pl.BlockSpec(memory_space=pltpu.SMEM)
        return pl.pallas_call(
            functools.partial(kernel, F, Z, F == 4),
            out_shape=(
                jax.ShapeDtypeStruct((1, T, HH), bf),
                jax.ShapeDtypeStruct((T, HD), bf),
            ),
            in_specs=[anywhere] * 6 + [smem, smem],
            out_specs=(pl.BlockSpec(memory_space=pltpu.VMEM),) * 2,
            scratch_shapes=[
                pltpu.VMEM((T, HH), bf),
                pltpu.VMEM((T, HH), bf),
                pltpu.VMEM(gate_table.shape, f32),
                pltpu.VMEM((Z, 2, T, HD), bf),
                pltpu.VMEM((Z, T, HD), bf),
                pltpu.VMEM((8, HH), f32),
                pltpu.VMEM((3, Z, 2, 2, T, HD), bf),
                pltpu.VMEM((Z, T, HD), bf),
                pltpu.VMEM((Z, T, HD), bf),
                pltpu.VMEM((Z, T, HD), bf),
                pltpu.VMEM((T, HD), bf),
                pltpu.VMEM((1, T, HH), bf),
                pltpu.VMEM((T, HD), bf),
                pltpu.VMEM((8, HH), f32),
                pltpu.VMEM((8, HD), f32),
                pltpu.VMEM((HD, Z * T), bf),
                pltpu.VMEM((8, Z * T), f32),
                pltpu.VMEM((8, Z * T), f32),
                pltpu.VMEM((HD, Z * T), f32),
                dma((3,)), dma((Z,)),
                dma((Z,)), dma((Z,)), dma((Z,)), dma((Z,)),
                dma((Z,)), dma((Z,)), dma((2, Z)), dma((2, Z)), dma((2, Z)), dma((2, Z)),
                dma((Z,)), dma((Z,)), dma,
                dma, dma, dma((F,)), dma,
                dma, dma, dma((F,)), dma,
                dma,
            ],
            compiler_params=pltpu.CompilerParams(
                collective_id=0, has_side_effects=True, vmem_limit_bytes=48 * 1024 * 1024
            ),
        )(
            *(pltpu.with_memory_space_constraint(x, pltpu.HBM) for x in blocks), timesteps, positions
        )

    placed = (
        P("frame", ("head", "tok"), None),
        P("frame", ("head", "tok"), None),
        P("frame", ("head", "tok"), None),
        P("frame", ("head", "tok"), None),
        P(("head", "tok"), None),
        P(),
        P("frame"),
        P("frame"),
    )
    return jax.shard_map(
        per_device,
        mesh=mesh,
        in_specs=placed,
        out_specs=(P("frame", ("head", "tok"), None), P(("head", "tok"), "frame")),
        check_vma=False,
    )
```

```python
import functools
import math

import jax
import jax.numpy as jnp
from jax import lax
from jax.experimental import pallas as pl
from jax.experimental.pallas import tpu as pltpu
from jax.sharding import PartitionSpec as P

HD = 128
HALF = 8
MESH = pl.DeviceIdType.MESH


def kernel(
    frames, heads, relay,
    q_hbm, k_hbm, v_hbm, res_hbm, inc_hbm, gate_hbm, steps_ref, pos_ref,
    nq_ref, lv_ref,
    q_in, k_in, gate_in, kv_out, q_out, gate_out,
    kv_buf, q_buf, o_out, o_buf, lo_buf, res_buf, lres_buf, gate_buf, lgate_buf,
    q_cols, stats, blended_buf, other_stats, other_blended,
    load_sem, v_sem, kvz_s, kvz_r, qz_s, qz_r, peer_s, peer_r, fr_s, fr_r, part_s, part_r,
    o_s, o_r, lo_r, res_s, res_r, lres_s, lres_r, gate_s, gate_r, lgate_s, lgate_r, out_sem,
):
    F, Z = frames, heads
    f = lax.axis_index("frame")
    h = lax.axis_index("head")
    t = lax.axis_index("tok")
    T = q_in.shape[0]
    has_prev = f > 0
    has_across = (f > 0) & (f < F - 1)
    partner = f + 1 - 2 * lax.rem(f, 2)
    across = f - 1 + 2 * lax.rem(f, 2)

    def at(fr, hd, tk):
        return {"frame": fr, "head": hd, "tok": tk}

    def remote(src, dst, send, recv, dev):
        return pltpu.make_async_remote_copy(
            src_ref=src, dst_ref=dst, send_sem=send, recv_sem=recv, device_id=dev, device_id_type=MESH
        )

    load_k = pltpu.make_async_copy(k_hbm.at[0], k_in, load_sem.at[0])
    load_q = pltpu.make_async_copy(q_hbm.at[0], q_in, load_sem.at[1])
    load_gate = pltpu.make_async_copy(gate_hbm, gate_in, load_sem.at[2])
    load_v = [
        pltpu.make_async_copy(v_hbm.at[0, :, pl.ds(j * HD, HD)], kv_out.at[j, 1], v_sem.at[j]) for j in range(Z)
    ]
    incoming = pltpu.make_async_copy(inc_hbm, nq_ref.at[0], out_sem)
    load_q.start()
    load_k.start()
    for c in load_v:
        c.start()
    load_gate.start()

    @pl.when(f == F - 1)
    def _():
        incoming.start()

    barrier = pltpu.get_barrier_semaphore()
    me = f * Z + h

    def greet(s, carry):
        other = lax.rem(me + s, F * Z)
        pl.semaphore_signal(barrier, inc=1, device_id=at(other // Z, lax.rem(other, Z), t), device_id_type=MESH)
        return carry

    lax.fori_loop(1, F * Z, greet, 0)
    pl.semaphore_signal(barrier, inc=1, device_id=at(f, h, 1 - t), device_id_type=MESH)

    lane = lax.broadcasted_iota(jnp.int32, (8, HD), 1)
    power = lax.rem(lane, HALF).astype(jnp.float32)
    angle = pos_ref[0].astype(jnp.float32) * jnp.exp2(-power)
    cosine = jnp.where(lane < 2 * HALF, jnp.cos(angle), 1.0)[0:1]
    sine = jnp.sin(angle)
    sine_up = jnp.where(lane < HALF, -sine, 0.0)[0:1]
    sine_down = jnp.where((lane >= HALF) & (lane < 2 * HALF), sine, 0.0)[0:1]

    def turned(x):
        x = x.astype(jnp.float32)
        up = pltpu.roll(x, HD - HALF, 1)
        down = pltpu.roll(x, HALF, 1)
        return (x * cosine + up * sine_up + down * sine_down).astype(jnp.bfloat16)

    load_q.wait()
    for j in range(Z):
        q_out[j] = turned(q_in[:, j * HD : (j + 1) * HD])
    load_k.wait()
    for j in range(Z):
        kv_out[j, 0] = turned(k_in[:, j * HD : (j + 1) * HD])
    for c in load_v:
        c.wait()
    pl.semaphore_wait(barrier, F * Z)

    def q_send(s):
        return remote(q_out.at[lax.rem(h + s, Z)], q_buf.at[0, s], qz_s.at[s], qz_r.at[s], at(f, lax.rem(h + s, Z), t))

    def kv_send(s):
        d = lax.rem(h + s, Z)
        return remote(kv_out.at[d], kv_buf.at[0, s], kvz_s.at[s], kvz_r.at[s], at(f, d, t))

    for s in range(1, Z):
        q_send(s).start()
    for s in range(1, Z):
        kv_send(s).start()

    def peer_send(s, src):
        return remote(src, q_buf.at[1, s], peer_s.at[s], peer_r.at[s], at(f, h, 1 - t))

    def pair_send(s, src):
        return remote(src, kv_buf.at[1, s], fr_s.at[0, s], fr_r.at[0, s], at(partner, h, t))

    def across_send(s, src):
        return remote(src, kv_buf.at[2, s], fr_s.at[1, s], fr_r.at[1, s], at(across, h, t))

    def relay_send(s):
        return remote(kv_buf.at[1, s], kv_buf.at[2, s], fr_s.at[1, s], fr_r.at[1, s], at(lax.rem(f + 2, F), h, t))

    def spread(s, src):
        pair_send(s, src).start()
        if not relay:

            @pl.when(has_across)
            def _():
                across_send(s, src).start()

    spread(0, kv_out.at[h])
    peer_send(0, q_out.at[h]).start()
    kv_buf[0, 0] = kv_out[h]
    q_buf[0, 0] = q_out[h]

    load_gate.wait()
    gate_out[...] = jnp.broadcast_to(gate_in[pl.ds(steps_ref[0], 1), :], gate_out.shape)

    def came(ref, sem):
        remote(ref, ref, sem, sem, at(f, h, 1 - t)).wait_recv()

    def take_queries(s):
        came(q_buf.at[0, s], qz_r.at[s])
        peer_send(s, q_buf.at[0, s]).start()

    def take_own(s):
        came(kv_buf.at[0, s], kvz_r.at[s])
        spread(s, kv_buf.at[0, s])

    def take_pair(s):
        came(kv_buf.at[1, s], fr_r.at[0, s])
        if relay:

            @pl.when(jnp.logical_not(has_across))
            def _():
                relay_send(s).start()

    def res_send():
        return remote(res_hbm, res_buf, res_s, res_r, at(f - 1, h, t))

    def gate_send():
        return remote(gate_out, gate_buf, gate_s, gate_r, at(f - 1, h, t))

    def lres_send(g):
        return remote(res_hbm.at[0, :, pl.ds(g * HD, HD)], lres_buf, lres_s.at[g], lres_r, at(g, h, t))

    def lgate_send(g):
        return remote(gate_out.at[:, pl.ds(g * HD, HD)], lgate_buf, lgate_s.at[g], lgate_r, at(g, h, t))

    def send_residual():
        @pl.when(has_prev)
        def _():
            res_send().start()
            gate_send().start()

        @pl.when(f == 0)
        def _():
            pltpu.make_async_copy(res_hbm.at[0, :, pl.ds(0, HD)], lres_buf, lres_r).start()
            pltpu.make_async_copy(gate_out.at[:, pl.ds(0, HD)], lgate_buf, lgate_r).start()
            for g in range(1, F):
                lres_send(g).start()
                lgate_send(g).start()

    rate = math.log2(math.e) / math.sqrt(HD)
    group = min(Z, 4)
    width = group * T

    def columns(i):
        return pl.ds(i * width, width)

    def turn_queries(i, carry):
        for half in range(2):
            rows = q_buf[half, pl.ds(i * group, group)].reshape(width, HD)
            q_cols[half, :, columns(i)] = rows.T
        return carry

    def merged(i, half, keys, values, first):
        scores = jnp.dot(keys, q_cols[half, :, columns(i)], preferred_element_type=jnp.float32)
        highest = jnp.max(scores, axis=0, keepdims=True)
        if not first:
            before = stats[half, 0, 0:1, columns(i)]
            highest = jnp.maximum(before, highest)
            keep = jnp.exp2((before - highest) * rate)
        weights = jnp.exp2((scores - highest) * rate)
        total = jnp.sum(weights, axis=0, keepdims=True)
        blended = jnp.dot(values, weights.astype(jnp.bfloat16), preferred_element_type=jnp.float32)
        if not first:
            total = stats[half, 1, 0:1, columns(i)] * keep + total
            blended = blended_buf[half, :, columns(i)] * keep + blended
        stats[half, 0, :, columns(i)] = jnp.broadcast_to(highest, (8, width))
        stats[half, 1, :, columns(i)] = jnp.broadcast_to(total, (8, width))
        blended_buf[half, :, columns(i)] = blended

    def block_pair(parts):
        keys = jnp.concatenate([kv_buf[p, s, 0] for p, s in parts])
        values = jnp.concatenate([kv_buf[p, s, 1] for p, s in parts])
        return keys, values.T

    def each_group(body):
        if Z == group:
            body(0, 0)
        else:
            lax.fori_loop(0, Z // group, body, 0)

    def gather(parts, first, between=None):
        keys, values = block_pair(parts)
        for half in (1, 0):

            def step(i, carry):
                merged(i, half, keys, values, first)
                return carry

            each_group(step)
            if half == 1 and between is not None:
                between()

    for s in range(Z):
        take_pair(s)
        if s == 0:
            for p in range(1, Z):
                take_queries(p)
        if s + 1 < Z:
            take_own(s + 1)
        if s == Z - 1:
            send_residual()
        if s == 1:
            for p in range(Z):
                came(q_buf.at[1, p], peer_r.at[p])
            each_group(turn_queries)
        if s % 2 == 1:
            gather([(0, s - 1), (1, s - 1), (0, s), (1, s)], s == 1)

    def partial_sends():
        return (
            remote(blended_buf.at[1], other_blended, part_s.at[0], part_r.at[0], at(f, h, 1 - t)),
            remote(stats.at[1], other_stats, part_s.at[1], part_r.at[1], at(f, h, 1 - t)),
        )

    def send_partial():
        for c in partial_sends():
            c.start()

    def o_send(s):
        return remote(o_out.at[s], o_buf.at[h], o_s.at[s], o_r.at[h], at(f - 1, lax.rem(h + Z - s, Z), t))

    def lo_send(s):
        return remote(o_out.at[s], lo_buf, o_s.at[s], lo_r, at(h, lax.rem(h + Z - s, Z), t))

    def leave(i, carry):
        mine, theirs = stats[0, 0, 0:1, columns(i)], other_stats[0, 0:1, columns(i)]
        highest = jnp.maximum(mine, theirs)
        mine, theirs = jnp.exp2((mine - highest) * rate), jnp.exp2((theirs - highest) * rate)
        total = mine * stats[0, 1, 0:1, columns(i)] + theirs * other_stats[1, 0:1, columns(i)]
        blended = mine * blended_buf[0, :, columns(i)] + theirs * other_blended[:, columns(i)]
        result = (blended / total).T.astype(jnp.bfloat16)
        for g in range(group):
            s = i * group + g
            o_out[s] = result[g * T : (g + 1) * T]

            @pl.when(f > 0)
            def _():
                o_send(s).start()

            @pl.when((f == 0) & ((h != 0) | (s != 0)))
            def _():
                lo_send(s).start()

            @pl.when((f == 0) & (h == 0) & (s == 0))
            def _():
                pltpu.make_async_copy(o_out.at[0], lo_buf, lo_r).start()

        return carry

    @pl.when(has_across)
    def _():
        for s in range(1, Z, 2):
            for p in (s - 1, s):
                came(kv_buf.at[2, p], fr_r.at[1, p])
            gather([(2, s - 1), (2, s)], False, send_partial if s == Z - 1 else None)

    @pl.when(jnp.logical_not(has_across))
    def _():
        send_partial()

    came(other_blended, part_r.at[0])
    came(other_stats, part_r.at[1])
    each_group(leave)

    came(lres_buf, lres_r)
    came(lgate_buf, lgate_r)
    came(lo_buf, lo_r)
    lv_ref[...] = (
        lres_buf[...].astype(jnp.float32) + lgate_buf[0:1, :] * lo_buf[...].astype(jnp.float32)
    ).astype(jnp.bfloat16)

    @pl.when(f < F - 1)
    def _():
        came(res_buf, res_r)
        came(gate_buf, gate_r)
        for j in range(Z):
            came(o_buf.at[j], o_r.at[j])
            cols = slice(j * HD, (j + 1) * HD)
            nq_ref[0, :, cols] = (
                res_buf[0, :, cols].astype(jnp.float32) + gate_buf[0:1, cols] * o_buf[j].astype(jnp.float32)
            ).astype(jnp.bfloat16)

    @pl.when(f == F - 1)
    def _():
        incoming.wait()

    for c in partial_sends():
        c.wait_send()
    for s in range(Z):
        if s > 0:
            kv_send(s).wait_send()
            q_send(s).wait_send()
        peer_send(s, q_out.at[0]).wait_send()
        pair_send(s, kv_out.at[0]).wait_send()
        if relay:

            @pl.when(jnp.logical_not(has_across))
            def _():
                relay_send(s).wait_send()

        else:

            @pl.when(has_across)
            def _():
                across_send(s, kv_out.at[0]).wait_send()

        @pl.when((f > 0) | (h != 0) | (s != 0))
        def _():
            o_send(s).wait_send()

    @pl.when(has_prev)
    def _():
        res_send().wait_send()
        gate_send().wait_send()

    @pl.when(f == 0)
    def _():
        for g in range(1, F):
            lres_send(g).wait_send()
            lgate_send(g).wait_send()


def solution(mesh):
    F, Z = mesh.shape["frame"], mesh.shape["head"]

    def per_device(queries, keys, values, residual, incoming, gate_table, timesteps, positions):
        T, HH = queries.shape[1], queries.shape[2]
        assert HH == Z * HD and HH == F * HD and mesh.shape["tok"] == 2
        blocks = (queries, keys, values, residual, incoming, gate_table)
        bf, f32 = jnp.bfloat16, jnp.float32
        dma = pltpu.SemaphoreType.DMA
        anywhere = pl.BlockSpec(memory_space=pl.ANY)
        smem = pl.BlockSpec(memory_space=pltpu.SMEM)
        return pl.pallas_call(
            functools.partial(kernel, F, Z, F == 4),
            out_shape=(
                jax.ShapeDtypeStruct((1, T, HH), bf),
                jax.ShapeDtypeStruct((T, HD), bf),
            ),
            in_specs=[anywhere] * 6 + [smem, smem],
            out_specs=(pl.BlockSpec(memory_space=pltpu.VMEM),) * 2,
            scratch_shapes=[
                pltpu.VMEM((T, HH), bf),
                pltpu.VMEM((T, HH), bf),
                pltpu.VMEM(gate_table.shape, f32),
                pltpu.VMEM((Z, 2, T, HD), bf),
                pltpu.VMEM((Z, T, HD), bf),
                pltpu.VMEM((8, HH), f32),
                pltpu.VMEM((3, Z, 2, T, HD), bf),
                pltpu.VMEM((2, Z, T, HD), bf),
                pltpu.VMEM((Z, T, HD), bf),
                pltpu.VMEM((Z, T, HD), bf),
                pltpu.VMEM((T, HD), bf),
                pltpu.VMEM((1, T, HH), bf),
                pltpu.VMEM((T, HD), bf),
                pltpu.VMEM((8, HH), f32),
                pltpu.VMEM((8, HD), f32),
                pltpu.VMEM((2, HD, Z * T), bf),
                pltpu.VMEM((2, 2, 8, Z * T), f32),
                pltpu.VMEM((2, HD, Z * T), f32),
                pltpu.VMEM((2, 8, Z * T), f32),
                pltpu.VMEM((HD, Z * T), f32),
                dma((3,)), dma((Z,)),
                dma((Z,)), dma((Z,)), dma((Z,)), dma((Z,)),
                dma((Z,)), dma((Z,)), dma((2, Z)), dma((2, Z)), dma((2,)), dma((2,)),
                dma((Z,)), dma((Z,)), dma,
                dma, dma, dma((F,)), dma,
                dma, dma, dma((F,)), dma,
                dma,
            ],
            compiler_params=pltpu.CompilerParams(
                collective_id=0, has_side_effects=True, vmem_limit_bytes=48 * 1024 * 1024
            ),
        )(
            *(pltpu.with_memory_space_constraint(x, pltpu.HBM) for x in blocks), timesteps, positions
        )

    placed = (
        P("frame", ("head", "tok"), None),
        P("frame", ("head", "tok"), None),
        P("frame", ("head", "tok"), None),
        P("frame", ("head", "tok"), None),
        P(("head", "tok"), None),
        P(),
        P("frame"),
        P("frame"),
    )
    return jax.shard_map(
        per_device,
        mesh=mesh,
        in_specs=placed,
        out_specs=(P("frame", ("head", "tok"), None), P(("head", "tok"), "frame")),
        check_vma=False,
    )
```

```python
import functools
import math

import jax
import jax.numpy as jnp
from jax import lax
from jax.experimental import pallas as pl
from jax.experimental.pallas import tpu as pltpu
from jax.sharding import PartitionSpec as P

HD = 128
HALF = 8
MESH = pl.DeviceIdType.MESH


def kernel(
    frames, heads, relay,
    q_hbm, k_hbm, v_hbm, res_hbm, inc_hbm, gate_hbm, steps_ref, pos_ref,
    nq_ref, lv_ref,
    q_in, k_in, gate_in, kv_out, q_out, gate_out,
    kv_buf, q_buf, o_out, o_buf, lo_buf, res_buf, lres_buf, gate_buf, lgate_buf,
    q_cols, top, weight_sum, blended_buf, q_relay, kv_relay,
    load_sem, v_sem, kvz_s, kvz_r, qz_s, qz_r, peer_s, peer_r, fr_s, fr_r, fwd_s, fwd_r,
    o_s, o_r, lo_r, res_s, res_r, lres_s, lres_r, gate_s, gate_r, lgate_s, lgate_r, out_sem,
):
    F, Z = frames, heads
    f = lax.axis_index("frame")
    h = lax.axis_index("head")
    t = lax.axis_index("tok")
    T = q_in.shape[0]
    has_prev = f > 0
    has_across = (f > 0) & (f < F - 1)
    partner = f + 1 - 2 * lax.rem(f, 2)
    across = f - 1 + 2 * lax.rem(f, 2)

    def at(fr, hd, tk):
        return {"frame": fr, "head": hd, "tok": tk}

    def remote(src, dst, send, recv, dev):
        return pltpu.make_async_remote_copy(
            src_ref=src, dst_ref=dst, send_sem=send, recv_sem=recv, device_id=dev, device_id_type=MESH
        )

    load_k = pltpu.make_async_copy(k_hbm.at[0], k_in, load_sem.at[0])
    load_q = pltpu.make_async_copy(q_hbm.at[0], q_in, load_sem.at[1])
    load_gate = pltpu.make_async_copy(gate_hbm, gate_in, load_sem.at[2])
    load_v = [
        pltpu.make_async_copy(v_hbm.at[0, :, pl.ds(j * HD, HD)], kv_out.at[j, 1], v_sem.at[j]) for j in range(Z)
    ]
    incoming = pltpu.make_async_copy(inc_hbm, nq_ref.at[0], out_sem)
    load_q.start()
    load_k.start()
    for c in load_v:
        c.start()
    load_gate.start()

    @pl.when(f == F - 1)
    def _():
        incoming.start()

    barrier = pltpu.get_barrier_semaphore()
    me = f * Z + h

    def greet(s, carry):
        other = lax.rem(me + s, F * Z)
        pl.semaphore_signal(barrier, inc=1, device_id=at(other // Z, lax.rem(other, Z), t), device_id_type=MESH)
        return carry

    lax.fori_loop(1, F * Z, greet, 0)
    pl.semaphore_signal(barrier, inc=1, device_id=at(f, h, 1 - t), device_id_type=MESH)

    lane = lax.broadcasted_iota(jnp.int32, (8, HD), 1)
    power = lax.rem(lane, HALF).astype(jnp.float32)
    angle = pos_ref[0].astype(jnp.float32) * jnp.exp2(-power)
    cosine = jnp.where(lane < 2 * HALF, jnp.cos(angle), 1.0)[0:1]
    sine = jnp.sin(angle)
    sine_up = jnp.where(lane < HALF, -sine, 0.0)[0:1]
    sine_down = jnp.where((lane >= HALF) & (lane < 2 * HALF), sine, 0.0)[0:1]

    def turned(x):
        x = x.astype(jnp.float32)
        up = pltpu.roll(x, HD - HALF, 1)
        down = pltpu.roll(x, HALF, 1)
        return (x * cosine + up * sine_up + down * sine_down).astype(jnp.bfloat16)

    load_q.wait()
    for j in range(Z):
        q_out[j] = turned(q_in[:, j * HD : (j + 1) * HD])
    load_k.wait()
    for j in range(Z):
        kv_out[j, 0] = turned(k_in[:, j * HD : (j + 1) * HD])
    for c in load_v:
        c.wait()
    pl.semaphore_wait(barrier, F * Z)

    hops = [(d, k) for k in range(Z - 1) for d in range(Z - 1, k, -1)]
    spot = {pair: n for n, pair in enumerate(hops)}
    both = (0, 1)

    def runs(d, k, way, place):
        return (place >= k) & (place - k + d < Z) if way == 0 else (place + k < Z) & (place + k >= d)

    def comes(d, k, way):
        return runs(d, k, way, h - 1) if way == 0 else runs(d, k, way, h + 1)

    def slot_of(place, d, way):
        nearer = jnp.minimum(place, d - 1) + jnp.minimum(Z - 1 - place, d - 1) + 1
        return nearer if way == 0 else nearer + (place >= d).astype(jnp.int32)

    def source_of(s):
        source = h
        for d in range(1, Z):
            source = jnp.where((h >= d) & (slot_of(h, d, 0) == s), h - d, source)
            source = jnp.where((h + d < Z) & (slot_of(h, d, 1) == s), h + d, source)
        return source

    def z_send(own, relayed, target, sems, d, k, way):
        step = 1 - 2 * way
        n = spot[d, k]
        dst = h + step * (d - k)
        block = own.at[dst] if k == 0 else relayed.at[way, spot[d, k - 1]]
        landing = target(slot_of(h + step, d, way)) if k == d - 1 else relayed.at[way, n]
        return remote(block, landing, sems[0].at[way, n], sems[1].at[way, n], at(f, h + step, t))

    def q_target(s):
        return q_buf.at[s]

    def kv_target(s):
        return kv_buf.at[0, s, t]

    def q_send(d, k, way):
        return z_send(q_out, q_relay, q_target, (qz_s, qz_r), d, k, way)

    def kv_send(d, k, way):
        return z_send(kv_out, kv_relay, kv_target, (kvz_s, kvz_r), d, k, way)

    def when_runs(d, k, way, send):
        @pl.when(runs(d, k, way, h))
        def _():
            send(d, k, way).start()

    for send in (q_send, kv_send):
        for d in range(Z - 1, 0, -1):
            for way in both:
                when_runs(d, 0, way, send)

    def peer_send(s, src):
        return remote(src, kv_buf.at[0, s, t], peer_s.at[s], peer_r.at[s], at(f, h, 1 - t))

    def pair_send(s, src):
        return remote(src, kv_buf.at[1, s, t], fr_s.at[0, s], fr_r.at[0, s], at(partner, h, t))

    def across_send(s, src):
        return remote(src, kv_buf.at[2, s, t], fr_s.at[1, s], fr_r.at[1, s], at(across, h, t))

    def relay_send(s):
        return remote(
            kv_buf.at[1, s, t], kv_buf.at[2, s, t], fr_s.at[1, s], fr_r.at[1, s], at(lax.rem(f + 2, F), h, t)
        )

    def fwd_send(slot, s):
        ref = kv_buf.at[slot, s, t]
        return remote(ref, ref, fwd_s.at[slot - 1, s], fwd_r.at[slot - 1, s], at(f, h, 1 - t))

    def spread(s, src):
        pair_send(s, src).start()
        if not relay:

            @pl.when(has_across)
            def _():
                across_send(s, src).start()

        peer_send(s, src).start()

    spread(0, kv_out.at[h])
    kv_buf[0, 0, t] = kv_out[h]
    q_buf[0] = q_out[h]

    load_gate.wait()
    gate_out[...] = jnp.broadcast_to(gate_in[pl.ds(steps_ref[0], 1), :], gate_out.shape)

    def came(ref, sem):
        remote(ref, ref, sem, sem, at(f, h, 1 - t)).wait_recv()

    def take(k, send, relayed, target, sem, arrived):
        for d in range(Z - 1, k, -1):
            for way in both:

                @pl.when(comes(d, k, way))
                def _():
                    if k == d - 1:
                        s = slot_of(h, d, way)
                        came(target(s), sem.at[way, spot[d, k]])
                        arrived(s)
                    else:
                        came(relayed.at[way, spot[d, k]], sem.at[way, spot[d, k]])
                        send(d, k + 1, way).start()

    def take_queries(k):
        take(k, q_send, q_relay, q_target, qz_r, lambda s: None)

    def take_own(k):
        take(k, kv_send, kv_relay, kv_target, kvz_r, lambda s: spread(s, kv_buf.at[0, s, t]))

    def take_pair(s):
        came(kv_buf.at[1, s, t], fr_r.at[0, s])
        if relay:

            @pl.when(jnp.logical_not(has_across))
            def _():
                relay_send(s).start()

        fwd_send(1, s).start()

    def take_across(s):
        @pl.when(has_across)
        def _():
            came(kv_buf.at[2, s, t], fr_r.at[1, s])
            fwd_send(2, s).start()

    def res_send():
        return remote(res_hbm, res_buf, res_s, res_r, at(f - 1, h, t))

    def gate_send():
        return remote(gate_out, gate_buf, gate_s, gate_r, at(f - 1, h, t))

    def lres_send(g):
        return remote(res_hbm.at[0, :, pl.ds(g * HD, HD)], lres_buf, lres_s.at[g], lres_r, at(g, h, t))

    def lgate_send(g):
        return remote(gate_out.at[:, pl.ds(g * HD, HD)], lgate_buf, lgate_s.at[g], lgate_r, at(g, h, t))

    def send_residual():
        @pl.when(has_prev)
        def _():
            res_send().start()
            gate_send().start()

        @pl.when(f == 0)
        def _():
            pltpu.make_async_copy(res_hbm.at[0, :, pl.ds(0, HD)], lres_buf, lres_r).start()
            pltpu.make_async_copy(gate_out.at[:, pl.ds(0, HD)], lgate_buf, lgate_r).start()
            for g in range(1, F):
                lres_send(g).start()
                lgate_send(g).start()

    rate = math.log2(math.e) / math.sqrt(HD)
    group = min(Z, 4)
    width = group * T

    def columns(i):
        return pl.ds(i * width, width)

    def turn_queries(i, carry):
        rows = q_buf[pl.ds(i * group, group)].reshape(width, HD)
        q_cols[:, columns(i)] = rows.T
        return carry

    def merged(i, keys, values, first):
        scores = jnp.dot(keys, q_cols[:, columns(i)], preferred_element_type=jnp.float32)
        highest = jnp.max(scores, axis=0, keepdims=True)
        if not first:
            before = top[0:1, columns(i)]
            highest = jnp.maximum(before, highest)
            keep = jnp.exp2((before - highest) * rate)
        weights = jnp.exp2((scores - highest) * rate)
        total = jnp.sum(weights, axis=0, keepdims=True)
        blended = jnp.dot(values, weights.astype(jnp.bfloat16), preferred_element_type=jnp.float32)
        if not first:
            total = weight_sum[0:1, columns(i)] * keep + total
            blended = blended_buf[:, columns(i)] * keep + blended
        return highest, total, blended

    def block_pair(parts):
        keys = jnp.concatenate([kv_buf[p, s, :, 0].reshape(2 * T, HD) for p, s in parts])
        values = jnp.concatenate([kv_buf[p, s, :, 1].reshape(2 * T, HD) for p, s in parts])
        return keys, values.T

    def each_group(body):
        if Z == group:
            body(0, 0)
        else:
            lax.fori_loop(0, Z // group, body, 0)

    def gather(parts, first):
        keys, values = block_pair(parts)

        def step(i, carry):
            highest, total, blended = merged(i, keys, values, first)
            top[0:1, columns(i)] = highest
            weight_sum[0:1, columns(i)] = total
            blended_buf[:, columns(i)] = blended
            return carry

        each_group(step)

    def near(s):
        came(kv_buf.at[0, s, 1 - t], peer_r.at[s])
        came(kv_buf.at[1, s, 1 - t], fwd_r.at[0, s])
        gather([(0, s), (1, s)], s == 0)

    def wait_across(s):
        for p in (s, s + 1):
            came(kv_buf.at[2, p, 1 - t], fwd_r.at[1, p])

    def far(s):
        @pl.when(has_across)
        def _():
            wait_across(s)
            gather([(2, s), (2, s + 1)], False)

    take_queries(0)
    for s in range(Z):
        if s + 2 < Z:
            take_queries(s + 1)
        if s + 1 < Z:
            take_own(s)
        take_pair(s)
        if s == Z - 1:
            send_residual()
        if s == 1:
            each_group(turn_queries)
        if s >= 1:
            near(s - 1)
        if s >= 2:
            take_across(s - 2)
        if s >= 3 and s % 2 == 1:
            far(s - 3)
    take_across(Z - 2)
    near(Z - 1)

    def o_send(s):
        return remote(o_out.at[s], o_buf.at[h], o_s.at[s], o_r.at[h], at(f - 1, source_of(s), t))

    def lo_send(s):
        return remote(o_out.at[s], lo_buf, o_s.at[s], lo_r, at(h, source_of(s), t))

    def leave_with(blended, total, i):
        result = (blended / total).T.astype(jnp.bfloat16)
        for g in range(group):
            s = i * group + g
            o_out[s] = result[g * T : (g + 1) * T]

            @pl.when(f > 0)
            def _():
                o_send(s).start()

            @pl.when((f == 0) & ((h != 0) | (s != 0)))
            def _():
                lo_send(s).start()

            @pl.when((f == 0) & (h == 0) & (s == 0))
            def _():
                pltpu.make_async_copy(o_out.at[0], lo_buf, lo_r).start()

    @pl.when(has_across)
    def _():
        came(kv_buf.at[2, Z - 1, t], fr_r.at[1, Z - 1])
        fwd_send(2, Z - 1).start()
        wait_across(Z - 2)
        keys, values = block_pair([(2, Z - 2), (2, Z - 1)])

        def last(i, carry):
            _, total, blended = merged(i, keys, values, False)
            leave_with(blended, total, i)
            return carry

        each_group(last)

    @pl.when(jnp.logical_not(has_across))
    def _():
        def last(i, carry):
            leave_with(blended_buf[:, columns(i)], weight_sum[0:1, columns(i)], i)
            return carry

        each_group(last)

    came(lres_buf, lres_r)
    came(lgate_buf, lgate_r)
    came(lo_buf, lo_r)
    lv_ref[...] = (
        lres_buf[...].astype(jnp.float32) + lgate_buf[0:1, :] * lo_buf[...].astype(jnp.float32)
    ).astype(jnp.bfloat16)

    @pl.when(f < F - 1)
    def _():
        came(res_buf, res_r)
        came(gate_buf, gate_r)
        for j in range(Z):
            came(o_buf.at[j], o_r.at[j])
            cols = slice(j * HD, (j + 1) * HD)
            nq_ref[0, :, cols] = (
                res_buf[0, :, cols].astype(jnp.float32) + gate_buf[0:1, cols] * o_buf[j].astype(jnp.float32)
            ).astype(jnp.bfloat16)

    @pl.when(f == F - 1)
    def _():
        incoming.wait()

    for d, k in hops:
        for way in both:

            @pl.when(runs(d, k, way, h))
            def _():
                q_send(d, k, way).wait_send()
                kv_send(d, k, way).wait_send()

    for s in range(Z):
        peer_send(s, kv_out.at[0]).wait_send()
        pair_send(s, kv_out.at[0]).wait_send()
        fwd_send(1, s).wait_send()

        @pl.when(has_across)
        def _():
            fwd_send(2, s).wait_send()

        if relay:

            @pl.when(jnp.logical_not(has_across))
            def _():
                relay_send(s).wait_send()

        else:

            @pl.when(has_across)
            def _():
                across_send(s, kv_out.at[0]).wait_send()

        @pl.when((f > 0) | (h != 0) | (s != 0))
        def _():
            o_send(s).wait_send()

    @pl.when(has_prev)
    def _():
        res_send().wait_send()
        gate_send().wait_send()

    @pl.when(f == 0)
    def _():
        for g in range(1, F):
            lres_send(g).wait_send()
            lgate_send(g).wait_send()


def solution(mesh):
    F, Z = mesh.shape["frame"], mesh.shape["head"]

    def per_device(queries, keys, values, residual, incoming, gate_table, timesteps, positions):
        T, HH = queries.shape[1], queries.shape[2]
        assert HH == Z * HD and HH == F * HD and mesh.shape["tok"] == 2
        blocks = (queries, keys, values, residual, incoming, gate_table)
        steps = Z * (Z - 1) // 2
        bf, f32 = jnp.bfloat16, jnp.float32
        dma = pltpu.SemaphoreType.DMA
        anywhere = pl.BlockSpec(memory_space=pl.ANY)
        smem = pl.BlockSpec(memory_space=pltpu.SMEM)
        return pl.pallas_call(
            functools.partial(kernel, F, Z, F == 4),
            out_shape=(
                jax.ShapeDtypeStruct((1, T, HH), bf),
                jax.ShapeDtypeStruct((T, HD), bf),
            ),
            in_specs=[anywhere] * 6 + [smem, smem],
            out_specs=(pl.BlockSpec(memory_space=pltpu.VMEM),) * 2,
            scratch_shapes=[
                pltpu.VMEM((T, HH), bf),
                pltpu.VMEM((T, HH), bf),
                pltpu.VMEM(gate_table.shape, f32),
                pltpu.VMEM((Z, 2, T, HD), bf),
                pltpu.VMEM((Z, T, HD), bf),
                pltpu.VMEM((8, HH), f32),
                pltpu.VMEM((3, Z, 2, 2, T, HD), bf),
                pltpu.VMEM((Z, T, HD), bf),
                pltpu.VMEM((Z, T, HD), bf),
                pltpu.VMEM((Z, T, HD), bf),
                pltpu.VMEM((T, HD), bf),
                pltpu.VMEM((1, T, HH), bf),
                pltpu.VMEM((T, HD), bf),
                pltpu.VMEM((8, HH), f32),
                pltpu.VMEM((8, HD), f32),
                pltpu.VMEM((HD, Z * T), bf),
                pltpu.VMEM((8, Z * T), f32),
                pltpu.VMEM((8, Z * T), f32),
                pltpu.VMEM((HD, Z * T), f32),
                pltpu.VMEM((2, steps, T, HD), bf),
                pltpu.VMEM((2, steps, 2, T, HD), bf),
                dma((3,)), dma((Z,)),
                dma((2, steps)), dma((2, steps)), dma((2, steps)), dma((2, steps)),
                dma((Z,)), dma((Z,)), dma((2, Z)), dma((2, Z)), dma((2, Z)), dma((2, Z)),
                dma((Z,)), dma((Z,)), dma,
                dma, dma, dma((F,)), dma,
                dma, dma, dma((F,)), dma,
                dma,
            ],
            compiler_params=pltpu.CompilerParams(
                collective_id=0, has_side_effects=True, vmem_limit_bytes=48 * 1024 * 1024
            ),
        )(
            *(pltpu.with_memory_space_constraint(x, pltpu.HBM) for x in blocks), timesteps, positions
        )

    placed = (
        P("frame", ("head", "tok"), None),
        P("frame", ("head", "tok"), None),
        P("frame", ("head", "tok"), None),
        P("frame", ("head", "tok"), None),
        P(("head", "tok"), None),
        P(),
        P("frame"),
        P("frame"),
    )
    return jax.shard_map(
        per_device,
        mesh=mesh,
        in_specs=placed,
        out_specs=(P("frame", ("head", "tok"), None), P(("head", "tok"), "frame")),
        check_vma=False,
    )
```

```python
import functools
import math

import jax
import jax.numpy as jnp
from jax import lax
from jax.experimental import pallas as pl
from jax.experimental.pallas import tpu as pltpu
from jax.sharding import PartitionSpec as P

HD = 128
HALF = 8
MESH = pl.DeviceIdType.MESH


def kernel(
    frames, heads, relay,
    q_hbm, k_hbm, v_hbm, res_hbm, inc_hbm, gate_hbm, steps_ref, pos_ref,
    nq_ref, lv_ref,
    q_in, k_in, gate_in, kv_out, q_out, gate_out,
    kv_buf, q_buf, o_out, o_buf, lo_buf, res_buf, lres_buf, gate_buf, lgate_buf,
    top, weight_sum, blended_buf,
    load_sem, v_sem, kvz_s, kvz_r, qz_s, qz_r, peer_s, peer_r, fr_s, fr_r, fwd_s, fwd_r,
    o_s, o_r, lo_r, res_s, res_r, lres_s, lres_r, gate_s, gate_r, lgate_s, lgate_r, out_sem,
):
    F, Z = frames, heads
    f = lax.axis_index("frame")
    h = lax.axis_index("head")
    t = lax.axis_index("tok")
    T = q_in.shape[0]
    has_prev = f > 0
    has_across = (f > 0) & (f < F - 1)
    partner = f + 1 - 2 * lax.rem(f, 2)
    across = f - 1 + 2 * lax.rem(f, 2)

    def at(fr, hd, tk):
        return {"frame": fr, "head": hd, "tok": tk}

    def remote(src, dst, send, recv, dev):
        return pltpu.make_async_remote_copy(
            src_ref=src, dst_ref=dst, send_sem=send, recv_sem=recv, device_id=dev, device_id_type=MESH
        )

    load_k = pltpu.make_async_copy(k_hbm.at[0], k_in, load_sem.at[0])
    load_q = pltpu.make_async_copy(q_hbm.at[0], q_in, load_sem.at[1])
    load_gate = pltpu.make_async_copy(gate_hbm, gate_in, load_sem.at[2])
    load_v = [
        pltpu.make_async_copy(v_hbm.at[0, :, pl.ds(j * HD, HD)], kv_out.at[j, 1], v_sem.at[j]) for j in range(Z)
    ]
    incoming = pltpu.make_async_copy(inc_hbm, nq_ref.at[0], out_sem)
    load_k.start()
    for c in load_v:
        c.start()
    load_q.start()
    load_gate.start()

    @pl.when(f == F - 1)
    def _():
        incoming.start()

    barrier = pltpu.get_barrier_semaphore()
    me = f * Z + h

    def greet(s, carry):
        other = lax.rem(me + s, F * Z)
        pl.semaphore_signal(barrier, inc=1, device_id=at(other // Z, lax.rem(other, Z), t), device_id_type=MESH)
        return carry

    lax.fori_loop(1, F * Z, greet, 0)
    pl.semaphore_signal(barrier, inc=1, device_id=at(f, h, 1 - t), device_id_type=MESH)

    lane = lax.broadcasted_iota(jnp.int32, (8, HD), 1)
    power = lax.rem(lane, HALF).astype(jnp.float32)
    angle = pos_ref[0].astype(jnp.float32) * jnp.exp2(-power)
    cosine = jnp.where(lane < 2 * HALF, jnp.cos(angle), 1.0)[0:1]
    sine = jnp.sin(angle)
    sine_up = jnp.where(lane < HALF, -sine, 0.0)[0:1]
    sine_down = jnp.where((lane >= HALF) & (lane < 2 * HALF), sine, 0.0)[0:1]

    def turned(x):
        x = x.astype(jnp.float32)
        up = pltpu.roll(x, HD - HALF, 1)
        down = pltpu.roll(x, HALF, 1)
        return (x * cosine + up * sine_up + down * sine_down).astype(jnp.bfloat16)

    load_k.wait()
    for j in range(Z):
        kv_out[j, 0] = turned(k_in[:, j * HD : (j + 1) * HD])
    for c in load_v:
        c.wait()
    pl.semaphore_wait(barrier, F * Z)

    def kv_send(s):
        d = lax.rem(h + s, Z)
        return remote(kv_out.at[d], kv_buf.at[0, t, h], kvz_s.at[s], kvz_r.at[s], at(f, d, t))

    def q_send(s):
        d = lax.rem(h + s, Z)
        return remote(q_out.at[d], q_buf.at[s], qz_s.at[s], qz_r.at[s], at(f, d, t))

    for s in range(1, Z):
        kv_send(s).start()

    def peer_send(s, b, src):
        return remote(src, kv_buf.at[0, t, b], peer_s.at[s], peer_r.at[s], at(f, h, 1 - t))

    def pair_send(s, b, src):
        return remote(src, kv_buf.at[1, t, b], fr_s.at[0, s], fr_r.at[0, s], at(partner, h, t))

    def across_send(s, b, src):
        return remote(src, kv_buf.at[2, t, b], fr_s.at[1, s], fr_r.at[1, s], at(across, h, t))

    def relay_send(s, b):
        return remote(
            kv_buf.at[1, t, b], kv_buf.at[2, t, b], fr_s.at[1, s], fr_r.at[1, s], at(lax.rem(f + 2, F), h, t)
        )

    def fwd_send(slot, s, b):
        ref = kv_buf.at[slot, t, b]
        return remote(ref, ref, fwd_s.at[slot - 1, s], fwd_r.at[slot - 1, s], at(f, h, 1 - t))

    def spread(s, b, src):
        pair_send(s, b, src).start()
        if not relay:

            @pl.when(has_across)
            def _():
                across_send(s, b, src).start()

        peer_send(s, b, src).start()

    spread(0, h, kv_out.at[h])
    load_q.wait()
    for j in range(Z):
        q_out[j] = turned(q_in[:, j * HD : (j + 1) * HD])
    for s in range(1, Z):
        q_send(s).start()
    kv_buf[0, t, h] = kv_out[h]
    q_buf[0] = q_out[h]

    load_gate.wait()
    gate_out[...] = jnp.broadcast_to(gate_in[pl.ds(steps_ref[0], 1), :], gate_out.shape)

    def came(ref, sem):
        remote(ref, ref, sem, sem, at(f, h, 1 - t)).wait_recv()

    def block(s):
        return lax.rem(h + Z - s, Z)

    def take_own(s):
        came(kv_buf.at[0, t, block(s)], kvz_r.at[s])
        spread(s, block(s), kv_buf.at[0, t, block(s)])

    def take_pair(s):
        came(kv_buf.at[1, t, block(s)], fr_r.at[0, s])
        if relay:

            @pl.when(jnp.logical_not(has_across))
            def _():
                relay_send(s, block(s)).start()

        fwd_send(1, s, block(s)).start()

    def take_across(s):
        @pl.when(has_across)
        def _():
            came(kv_buf.at[2, t, block(s)], fr_r.at[1, s])
            fwd_send(2, s, block(s)).start()

    def res_send():
        return remote(res_hbm, res_buf, res_s, res_r, at(f - 1, h, t))

    def gate_send():
        return remote(gate_out, gate_buf, gate_s, gate_r, at(f - 1, h, t))

    def lres_send(g):
        return remote(res_hbm.at[0, :, pl.ds(g * HD, HD)], lres_buf, lres_s.at[g], lres_r, at(g, h, t))

    def lgate_send(g):
        return remote(gate_out.at[:, pl.ds(g * HD, HD)], lgate_buf, lgate_s.at[g], lgate_r, at(g, h, t))

    def send_residual():
        @pl.when(has_prev)
        def _():
            res_send().start()
            gate_send().start()

        @pl.when(f == 0)
        def _():
            pltpu.make_async_copy(res_hbm.at[0, :, pl.ds(0, HD)], lres_buf, lres_r).start()
            pltpu.make_async_copy(gate_out.at[:, pl.ds(0, HD)], lgate_buf, lgate_r).start()
            for g in range(1, F):
                lres_send(g).start()
                lgate_send(g).start()

    for s in range(Z):
        take_pair(s)
        if s + 1 < Z:
            take_own(s + 1)
        if s == Z - 2:
            send_residual()
        if s >= 1:
            take_across(s - 1)

    for s in range(Z):
        b = lax.rem(h + s, Z)
        came(kv_buf.at[0, 1 - t, b], peer_r.at[s])

    rate = math.log2(math.e) / math.sqrt(HD)
    keys_all = 2 * Z * T
    group = 2 if Z <= 4 else 1

    def score(rows, slot):
        return lax.dot_general(
            rows,
            kv_buf[slot, :, :, 0].reshape(keys_all, HD),
            (((1,), (1,)), ((), ())),
            preferred_element_type=jnp.float32,
        )

    def blend(weights, slot):
        return jnp.dot(
            weights.astype(jnp.bfloat16),
            kv_buf[slot, :, :, 1].reshape(keys_all, HD),
            preferred_element_type=jnp.float32,
        )

    def near(i, first):
        rows = q_buf[pl.ds(i * group, group)].reshape(group * T, HD)
        own = score(rows, 0)
        if first:
            for s in range(Z):
                b = lax.rem(h + s, Z)
                came(kv_buf.at[1, 1 - t, b], fwd_r.at[0, s])
        beside = score(rows, 1)
        highest = jnp.maximum(jnp.max(own, axis=1, keepdims=True), jnp.max(beside, axis=1, keepdims=True))
        own = jnp.exp2((own - highest) * rate)
        beside = jnp.exp2((beside - highest) * rate)
        at_rows = pl.ds(i * group * T, group * T)
        top[at_rows] = jnp.broadcast_to(highest, (group * T, HD))
        total = jnp.sum(own, axis=1, keepdims=True) + jnp.sum(beside, axis=1, keepdims=True)
        weight_sum[at_rows] = jnp.broadcast_to(total, (group * T, HD))
        blended_buf[at_rows] = blend(own, 0) + blend(beside, 1)

    def take_queries(i):
        for s in range(max(i * group, 1), (i + 1) * group):
            came(q_buf.at[s], qz_r.at[s])

    def finish_across():
        take_across(Z - 1)

        @pl.when(has_across)
        def _():
            for s in range(Z):
                came(kv_buf.at[2, 1 - t, block(s)], fwd_r.at[1, s])

    def o_send(s):
        return remote(o_out.at[s], o_buf.at[h], o_s.at[s], o_r.at[h], at(f - 1, lax.rem(h + Z - s, Z), t))

    def lo_send(s):
        return remote(o_out.at[s], lo_buf, o_s.at[s], lo_r, at(h, lax.rem(h + Z - s, Z), t))

    def leave_with(result, i):
        for g in range(group):
            s = i * group + g
            o_out[s] = result[g * T : (g + 1) * T]

            @pl.when(f > 0)
            def _():
                o_send(s).start()

            @pl.when((f == 0) & ((h != 0) | (s != 0)))
            def _():
                lo_send(s).start()

            @pl.when((f == 0) & (h == 0) & (s == 0))
            def _():
                pltpu.make_async_copy(o_out.at[0], lo_buf, lo_r).start()

    def finish(i, carry):
        at_rows = pl.ds(i * group * T, group * T)

        @pl.when(has_across)
        def _():
            scores = score(q_buf[pl.ds(i * group, group)].reshape(group * T, HD), 2)
            before = top[at_rows]
            highest = jnp.maximum(before, jnp.max(scores, axis=1, keepdims=True))
            keep = jnp.exp2((before - highest) * rate)
            weights = jnp.exp2((scores - highest[:, 0:1]) * rate)
            total = weight_sum[at_rows] * keep + jnp.sum(weights, axis=1, keepdims=True)
            leave_with(((blended_buf[at_rows] * keep + blend(weights, 2)) / total).astype(jnp.bfloat16), i)

        @pl.when(jnp.logical_not(has_across))
        def _():
            leave_with((blended_buf[at_rows] / weight_sum[at_rows]).astype(jnp.bfloat16), i)

        return carry

    if Z <= 4:
        for i in range(Z // group):
            take_queries(i)
            near(i, i == 0)
            if i == 0:
                finish_across()
            finish(i, 0)
    else:
        for i in range(Z // group):
            take_queries(i)
        near(0, True)
        finish_across()
        lax.fori_loop(1, Z // group, lambda i, c: (near(i, False), c)[1], 0)
        lax.fori_loop(0, Z // group, finish, 0)

    came(lres_buf, lres_r)
    came(lgate_buf, lgate_r)
    came(lo_buf, lo_r)
    lv_ref[...] = (
        lres_buf[...].astype(jnp.float32) + lgate_buf[0:1, :] * lo_buf[...].astype(jnp.float32)
    ).astype(jnp.bfloat16)

    @pl.when(f < F - 1)
    def _():
        came(res_buf, res_r)
        came(gate_buf, gate_r)
        for j in range(Z):
            came(o_buf.at[j], o_r.at[j])
            cols = slice(j * HD, (j + 1) * HD)
            nq_ref[0, :, cols] = (
                res_buf[0, :, cols].astype(jnp.float32) + gate_buf[0:1, cols] * o_buf[j].astype(jnp.float32)
            ).astype(jnp.bfloat16)

    @pl.when(f == F - 1)
    def _():
        incoming.wait()

    for s in range(Z):
        if s > 0:
            kv_send(s).wait_send()
            q_send(s).wait_send()
        peer_send(s, 0, kv_out.at[0]).wait_send()
        pair_send(s, 0, kv_out.at[0]).wait_send()
        fwd_send(1, s, 0).wait_send()

        @pl.when(has_across)
        def _():
            fwd_send(2, s, 0).wait_send()

        if relay:

            @pl.when(jnp.logical_not(has_across))
            def _():
                relay_send(s, 0).wait_send()

        else:

            @pl.when(has_across)
            def _():
                across_send(s, 0, kv_out.at[0]).wait_send()

        @pl.when((f > 0) | (h != 0) | (s != 0))
        def _():
            o_send(s).wait_send()

    @pl.when(has_prev)
    def _():
        res_send().wait_send()
        gate_send().wait_send()

    @pl.when(f == 0)
    def _():
        for g in range(1, F):
            lres_send(g).wait_send()
            lgate_send(g).wait_send()


def solution(mesh):
    F, Z = mesh.shape["frame"], mesh.shape["head"]

    def per_device(queries, keys, values, residual, incoming, gate_table, timesteps, positions):
        T, HH = queries.shape[1], queries.shape[2]
        assert HH == Z * HD and HH == F * HD and mesh.shape["tok"] == 2
        blocks = (queries, keys, values, residual, incoming, gate_table)
        bf, f32 = jnp.bfloat16, jnp.float32
        dma = pltpu.SemaphoreType.DMA
        anywhere = pl.BlockSpec(memory_space=pl.ANY)
        smem = pl.BlockSpec(memory_space=pltpu.SMEM)
        return pl.pallas_call(
            functools.partial(kernel, F, Z, F == 4),
            out_shape=(
                jax.ShapeDtypeStruct((1, T, HH), bf),
                jax.ShapeDtypeStruct((T, HD), bf),
            ),
            in_specs=[anywhere] * 6 + [smem, smem],
            out_specs=(pl.BlockSpec(memory_space=pltpu.VMEM),) * 2,
            scratch_shapes=[
                pltpu.VMEM((T, HH), bf),
                pltpu.VMEM((T, HH), bf),
                pltpu.VMEM(gate_table.shape, f32),
                pltpu.VMEM((Z, 2, T, HD), bf),
                pltpu.VMEM((Z, T, HD), bf),
                pltpu.VMEM((8, HH), f32),
                pltpu.VMEM((3, 2, Z, 2, T, HD), bf),
                pltpu.VMEM((Z, T, HD), bf),
                pltpu.VMEM((Z, T, HD), bf),
                pltpu.VMEM((Z, T, HD), bf),
                pltpu.VMEM((T, HD), bf),
                pltpu.VMEM((1, T, HH), bf),
                pltpu.VMEM((T, HD), bf),
                pltpu.VMEM((8, HH), f32),
                pltpu.VMEM((8, HD), f32),
                pltpu.VMEM((Z * T, HD), f32),
                pltpu.VMEM((Z * T, HD), f32),
                pltpu.VMEM((Z * T, HD), f32),
                dma((3,)), dma((Z,)),
                dma((Z,)), dma((Z,)), dma((Z,)), dma((Z,)),
                dma((Z,)), dma((Z,)), dma((2, Z)), dma((2, Z)), dma((2, Z)), dma((2, Z)),
                dma((Z,)), dma((Z,)), dma,
                dma, dma, dma((F,)), dma,
                dma, dma, dma((F,)), dma,
                dma,
            ],
            compiler_params=pltpu.CompilerParams(
                collective_id=0, has_side_effects=True, vmem_limit_bytes=48 * 1024 * 1024
            ),
        )(
            *(pltpu.with_memory_space_constraint(x, pltpu.HBM) for x in blocks), timesteps, positions
        )

    placed = (
        P("frame", ("head", "tok"), None),
        P("frame", ("head", "tok"), None),
        P("frame", ("head", "tok"), None),
        P("frame", ("head", "tok"), None),
        P(("head", "tok"), None),
        P(),
        P("frame"),
        P("frame"),
    )
    return jax.shard_map(
        per_device,
        mesh=mesh,
        in_specs=placed,
        out_specs=(P("frame", ("head", "tok"), None), P(("head", "tok"), "frame")),
        check_vma=False,
    )
```

```python
import functools
import math

import jax
import jax.numpy as jnp
from jax import lax
from jax.experimental import pallas as pl
from jax.experimental.pallas import tpu as pltpu
from jax.sharding import PartitionSpec as P

HD = 128
HALF = 8
MESH = pl.DeviceIdType.MESH


def kernel(
    frames, heads, relay,
    q_hbm, k_hbm, v_hbm, res_hbm, inc_hbm, gate_hbm, steps_ref, pos_ref,
    nq_ref, lv_ref,
    q_in, k_in, gate_in, kv_out, q_out, gate_out,
    kv_buf, q_buf, o_out, o_buf, lo_buf, res_buf, lres_buf, gate_buf, lgate_buf,
    top, weight_sum, blended_buf,
    load_sem, v_sem, kvz_s, kvz_r, qz_s, qz_r, peer_s, peer_r, fr_s, fr_r, fwd_s, fwd_r,
    o_s, o_r, lo_r, res_s, res_r, lres_s, lres_r, gate_s, gate_r, lgate_s, lgate_r, out_sem,
):
    F, Z = frames, heads
    f = lax.axis_index("frame")
    h = lax.axis_index("head")
    t = lax.axis_index("tok")
    T = q_in.shape[0]
    has_prev = f > 0
    has_across = (f > 0) & (f < F - 1)
    partner = f + 1 - 2 * lax.rem(f, 2)
    across = f - 1 + 2 * lax.rem(f, 2)

    def at(fr, hd, tk):
        return {"frame": fr, "head": hd, "tok": tk}

    def remote(src, dst, send, recv, dev):
        return pltpu.make_async_remote_copy(
            src_ref=src, dst_ref=dst, send_sem=send, recv_sem=recv, device_id=dev, device_id_type=MESH
        )

    load_k = pltpu.make_async_copy(k_hbm.at[0], k_in, load_sem.at[0])
    load_q = pltpu.make_async_copy(q_hbm.at[0], q_in, load_sem.at[1])
    load_gate = pltpu.make_async_copy(gate_hbm, gate_in, load_sem.at[2])
    load_v = [
        pltpu.make_async_copy(v_hbm.at[0, :, pl.ds(j * HD, HD)], kv_out.at[j, 1], v_sem.at[j]) for j in range(Z)
    ]
    incoming = pltpu.make_async_copy(inc_hbm, nq_ref.at[0], out_sem)
    load_k.start()
    for c in load_v:
        c.start()
    load_q.start()
    load_gate.start()

    @pl.when(f == F - 1)
    def _():
        incoming.start()

    barrier = pltpu.get_barrier_semaphore()
    me = f * Z + h

    def greet(s, carry):
        other = lax.rem(me + s, F * Z)
        pl.semaphore_signal(barrier, inc=1, device_id=at(other // Z, lax.rem(other, Z), t), device_id_type=MESH)
        return carry

    lax.fori_loop(1, F * Z, greet, 0)
    pl.semaphore_signal(barrier, inc=1, device_id=at(f, h, 1 - t), device_id_type=MESH)

    lane = lax.broadcasted_iota(jnp.int32, (8, HD), 1)
    power = lax.rem(lane, HALF).astype(jnp.float32)
    angle = pos_ref[0].astype(jnp.float32) * jnp.exp2(-power)
    cosine = jnp.where(lane < 2 * HALF, jnp.cos(angle), 1.0)[0:1]
    sine = jnp.sin(angle)
    sine_up = jnp.where(lane < HALF, -sine, 0.0)[0:1]
    sine_down = jnp.where((lane >= HALF) & (lane < 2 * HALF), sine, 0.0)[0:1]

    def turned(x):
        x = x.astype(jnp.float32)
        up = pltpu.roll(x, HD - HALF, 1)
        down = pltpu.roll(x, HALF, 1)
        return (x * cosine + up * sine_up + down * sine_down).astype(jnp.bfloat16)

    load_k.wait()
    for j in range(Z):
        kv_out[j, 0] = turned(k_in[:, j * HD : (j + 1) * HD])
    for c in load_v:
        c.wait()
    pl.semaphore_wait(barrier, F * Z)

    def kv_send(s):
        d = lax.rem(h + s, Z)
        return remote(kv_out.at[d], kv_buf.at[0, t, h], kvz_s.at[s], kvz_r.at[s], at(f, d, t))

    def q_send(s):
        d = lax.rem(h + s, Z)
        return remote(q_out.at[d], q_buf.at[s], qz_s.at[s], qz_r.at[s], at(f, d, t))

    for s in range(1, Z):
        kv_send(s).start()

    def peer_send(s, b, src):
        return remote(src, kv_buf.at[0, t, b], peer_s.at[s], peer_r.at[s], at(f, h, 1 - t))

    def pair_send(s, b, src):
        return remote(src, kv_buf.at[1, t, b], fr_s.at[0, s], fr_r.at[0, s], at(partner, h, t))

    def across_send(s, b, src):
        return remote(src, kv_buf.at[2, t, b], fr_s.at[1, s], fr_r.at[1, s], at(across, h, t))

    def relay_send(s, b):
        return remote(
            kv_buf.at[1, t, b], kv_buf.at[2, t, b], fr_s.at[1, s], fr_r.at[1, s], at(lax.rem(f + 2, F), h, t)
        )

    def fwd_send(slot, s, b):
        ref = kv_buf.at[slot, t, b]
        return remote(ref, ref, fwd_s.at[slot - 1, s], fwd_r.at[slot - 1, s], at(f, h, 1 - t))

    def spread(s, b, src):
        pair_send(s, b, src).start()
        if not relay:

            @pl.when(has_across)
            def _():
                across_send(s, b, src).start()

        peer_send(s, b, src).start()

    spread(0, h, kv_out.at[h])
    load_q.wait()
    for j in range(Z):
        q_out[j] = turned(q_in[:, j * HD : (j + 1) * HD])
    for s in range(1, Z):
        q_send(s).start()
    kv_buf[0, t, h] = kv_out[h]
    q_buf[0] = q_out[h]

    load_gate.wait()
    gate_out[...] = jnp.broadcast_to(gate_in[pl.ds(steps_ref[0], 1), :], gate_out.shape)

    def came(ref, sem):
        remote(ref, ref, sem, sem, at(f, h, 1 - t)).wait_recv()

    def block(s):
        return lax.rem(h + Z - s, Z)

    def take_own(s):
        came(kv_buf.at[0, t, block(s)], kvz_r.at[s])
        spread(s, block(s), kv_buf.at[0, t, block(s)])

    def take_pair(s):
        came(kv_buf.at[1, t, block(s)], fr_r.at[0, s])
        if relay:

            @pl.when(jnp.logical_not(has_across))
            def _():
                relay_send(s, block(s)).start()

        fwd_send(1, s, block(s)).start()

    def take_across(s):
        @pl.when(has_across)
        def _():
            came(kv_buf.at[2, t, block(s)], fr_r.at[1, s])
            fwd_send(2, s, block(s)).start()

    def res_send():
        return remote(res_hbm, res_buf, res_s, res_r, at(f - 1, h, t))

    def gate_send():
        return remote(gate_out, gate_buf, gate_s, gate_r, at(f - 1, h, t))

    def lres_send(g):
        return remote(res_hbm.at[0, :, pl.ds(g * HD, HD)], lres_buf, lres_s.at[g], lres_r, at(g, h, t))

    def lgate_send(g):
        return remote(gate_out.at[:, pl.ds(g * HD, HD)], lgate_buf, lgate_s.at[g], lgate_r, at(g, h, t))

    def send_residual():
        @pl.when(has_prev)
        def _():
            res_send().start()
            gate_send().start()

        @pl.when(f == 0)
        def _():
            pltpu.make_async_copy(res_hbm.at[0, :, pl.ds(0, HD)], lres_buf, lres_r).start()
            pltpu.make_async_copy(gate_out.at[:, pl.ds(0, HD)], lgate_buf, lgate_r).start()
            for g in range(1, F):
                lres_send(g).start()
                lgate_send(g).start()

    for s in range(1, Z):
        take_own(s)
    for s in range(Z):
        take_pair(s)
    send_residual()

    for s in range(Z):
        b = lax.rem(h + s, Z)
        came(kv_buf.at[0, 1 - t, b], peer_r.at[s])

    rate = math.log2(math.e) / math.sqrt(HD)
    keys_all = 2 * Z * T
    group = 2 if Z <= 4 else 1

    def score(rows, slot):
        return lax.dot_general(
            rows,
            kv_buf[slot, :, :, 0].reshape(keys_all, HD),
            (((1,), (1,)), ((), ())),
            preferred_element_type=jnp.float32,
        )

    def blend(weights, slot):
        return jnp.dot(
            weights.astype(jnp.bfloat16),
            kv_buf[slot, :, :, 1].reshape(keys_all, HD),
            preferred_element_type=jnp.float32,
        )

    def near(i, first):
        rows = q_buf[pl.ds(i * group, group)].reshape(group * T, HD)
        own = score(rows, 0)
        if first:
            for s in range(Z):
                b = lax.rem(h + s, Z)
                came(kv_buf.at[1, 1 - t, b], fwd_r.at[0, s])
        beside = score(rows, 1)
        highest = jnp.maximum(jnp.max(own, axis=1, keepdims=True), jnp.max(beside, axis=1, keepdims=True))
        own = jnp.exp2((own - highest) * rate)
        beside = jnp.exp2((beside - highest) * rate)
        at_rows = pl.ds(i * group * T, group * T)
        top[at_rows] = jnp.broadcast_to(highest, (group * T, HD))
        total = jnp.sum(own, axis=1, keepdims=True) + jnp.sum(beside, axis=1, keepdims=True)
        weight_sum[at_rows] = jnp.broadcast_to(total, (group * T, HD))
        blended_buf[at_rows] = blend(own, 0) + blend(beside, 1)

    def take_queries(i):
        for s in range(max(i * group, 1), (i + 1) * group):
            came(q_buf.at[s], qz_r.at[s])

    def finish_across():
        for s in range(Z):
            take_across(s)

        @pl.when(has_across)
        def _():
            for s in range(Z):
                came(kv_buf.at[2, 1 - t, block(s)], fwd_r.at[1, s])

    def o_send(s):
        return remote(o_out.at[s], o_buf.at[h], o_s.at[s], o_r.at[h], at(f - 1, lax.rem(h + Z - s, Z), t))

    def lo_send(s):
        return remote(o_out.at[s], lo_buf, o_s.at[s], lo_r, at(h, lax.rem(h + Z - s, Z), t))

    def leave_with(result, i):
        for g in range(group):
            s = i * group + g
            o_out[s] = result[g * T : (g + 1) * T]

            @pl.when(f > 0)
            def _():
                o_send(s).start()

            @pl.when((f == 0) & ((h != 0) | (s != 0)))
            def _():
                lo_send(s).start()

            @pl.when((f == 0) & (h == 0) & (s == 0))
            def _():
                pltpu.make_async_copy(o_out.at[0], lo_buf, lo_r).start()

    def finish(i, carry):
        at_rows = pl.ds(i * group * T, group * T)

        @pl.when(has_across)
        def _():
            scores = score(q_buf[pl.ds(i * group, group)].reshape(group * T, HD), 2)
            before = top[at_rows]
            highest = jnp.maximum(before, jnp.max(scores, axis=1, keepdims=True))
            keep = jnp.exp2((before - highest) * rate)
            weights = jnp.exp2((scores - highest[:, 0:1]) * rate)
            total = weight_sum[at_rows] * keep + jnp.sum(weights, axis=1, keepdims=True)
            leave_with(((blended_buf[at_rows] * keep + blend(weights, 2)) / total).astype(jnp.bfloat16), i)

        @pl.when(jnp.logical_not(has_across))
        def _():
            leave_with((blended_buf[at_rows] / weight_sum[at_rows]).astype(jnp.bfloat16), i)

        return carry

    if Z <= 4:
        for i in range(Z // group):
            take_queries(i)
            near(i, i == 0)
        finish_across()
        for i in range(Z // group):
            finish(i, 0)
    else:
        for i in range(Z // group):
            take_queries(i)
        near(0, True)
        finish_across()
        lax.fori_loop(1, Z // group, lambda i, c: (near(i, False), c)[1], 0)
        lax.fori_loop(0, Z // group, finish, 0)

    came(lres_buf, lres_r)
    came(lgate_buf, lgate_r)
    came(lo_buf, lo_r)
    lv_ref[...] = (
        lres_buf[...].astype(jnp.float32) + lgate_buf[0:1, :] * lo_buf[...].astype(jnp.float32)
    ).astype(jnp.bfloat16)

    @pl.when(f < F - 1)
    def _():
        came(res_buf, res_r)
        came(gate_buf, gate_r)
        for j in range(Z):
            came(o_buf.at[j], o_r.at[j])
            cols = slice(j * HD, (j + 1) * HD)
            nq_ref[0, :, cols] = (
                res_buf[0, :, cols].astype(jnp.float32) + gate_buf[0:1, cols] * o_buf[j].astype(jnp.float32)
            ).astype(jnp.bfloat16)

    @pl.when(f == F - 1)
    def _():
        incoming.wait()

    for s in range(Z):
        if s > 0:
            kv_send(s).wait_send()
            q_send(s).wait_send()
        peer_send(s, 0, kv_out.at[0]).wait_send()
        pair_send(s, 0, kv_out.at[0]).wait_send()
        fwd_send(1, s, 0).wait_send()

        @pl.when(has_across)
        def _():
            fwd_send(2, s, 0).wait_send()

        if relay:

            @pl.when(jnp.logical_not(has_across))
            def _():
                relay_send(s, 0).wait_send()

        else:

            @pl.when(has_across)
            def _():
                across_send(s, 0, kv_out.at[0]).wait_send()

        @pl.when((f > 0) | (h != 0) | (s != 0))
        def _():
            o_send(s).wait_send()

    @pl.when(has_prev)
    def _():
        res_send().wait_send()
        gate_send().wait_send()

    @pl.when(f == 0)
    def _():
        for g in range(1, F):
            lres_send(g).wait_send()
            lgate_send(g).wait_send()


def solution(mesh):
    F, Z = mesh.shape["frame"], mesh.shape["head"]

    def per_device(queries, keys, values, residual, incoming, gate_table, timesteps, positions):
        T, HH = queries.shape[1], queries.shape[2]
        assert HH == Z * HD and HH == F * HD and mesh.shape["tok"] == 2
        blocks = (queries, keys, values, residual, incoming, gate_table)
        bf, f32 = jnp.bfloat16, jnp.float32
        dma = pltpu.SemaphoreType.DMA
        anywhere = pl.BlockSpec(memory_space=pl.ANY)
        smem = pl.BlockSpec(memory_space=pltpu.SMEM)
        return pl.pallas_call(
            functools.partial(kernel, F, Z, F == 4),
            out_shape=(
                jax.ShapeDtypeStruct((1, T, HH), bf),
                jax.ShapeDtypeStruct((T, HD), bf),
            ),
            in_specs=[anywhere] * 6 + [smem, smem],
            out_specs=(pl.BlockSpec(memory_space=pltpu.VMEM),) * 2,
            scratch_shapes=[
                pltpu.VMEM((T, HH), bf),
                pltpu.VMEM((T, HH), bf),
                pltpu.VMEM(gate_table.shape, f32),
                pltpu.VMEM((Z, 2, T, HD), bf),
                pltpu.VMEM((Z, T, HD), bf),
                pltpu.VMEM((8, HH), f32),
                pltpu.VMEM((3, 2, Z, 2, T, HD), bf),
                pltpu.VMEM((Z, T, HD), bf),
                pltpu.VMEM((Z, T, HD), bf),
                pltpu.VMEM((Z, T, HD), bf),
                pltpu.VMEM((T, HD), bf),
                pltpu.VMEM((1, T, HH), bf),
                pltpu.VMEM((T, HD), bf),
                pltpu.VMEM((8, HH), f32),
                pltpu.VMEM((8, HD), f32),
                pltpu.VMEM((Z * T, HD), f32),
                pltpu.VMEM((Z * T, HD), f32),
                pltpu.VMEM((Z * T, HD), f32),
                dma((3,)), dma((Z,)),
                dma((Z,)), dma((Z,)), dma((Z,)), dma((Z,)),
                dma((Z,)), dma((Z,)), dma((2, Z)), dma((2, Z)), dma((2, Z)), dma((2, Z)),
                dma((Z,)), dma((Z,)), dma,
                dma, dma, dma((F,)), dma,
                dma, dma, dma((F,)), dma,
                dma,
            ],
            compiler_params=pltpu.CompilerParams(
                collective_id=0, has_side_effects=True, vmem_limit_bytes=48 * 1024 * 1024
            ),
        )(
            *(pltpu.with_memory_space_constraint(x, pltpu.HBM) for x in blocks), timesteps, positions
        )

    placed = (
        P("frame", ("head", "tok"), None),
        P("frame", ("head", "tok"), None),
        P("frame", ("head", "tok"), None),
        P("frame", ("head", "tok"), None),
        P(("head", "tok"), None),
        P(),
        P("frame"),
        P("frame"),
    )
    return jax.shard_map(
        per_device,
        mesh=mesh,
        in_specs=placed,
        out_specs=(P("frame", ("head", "tok"), None), P(("head", "tok"), "frame")),
        check_vma=False,
    )
```

```python
import functools
import math

import jax
import jax.numpy as jnp
from jax import lax
from jax.experimental import pallas as pl
from jax.experimental.pallas import tpu as pltpu
from jax.sharding import PartitionSpec as P

HD = 128
HALF = 8
MESH = pl.DeviceIdType.MESH


def kernel(
    frames, heads, relay,
    q_hbm, k_hbm, v_hbm, res_hbm, inc_hbm, gate_hbm, steps_ref, pos_ref,
    nq_ref, lv_ref,
    q_in, k_in, gate_in, kv_out, q_out, gate_out,
    kv_buf, q_buf, o_out, o_buf, lo_buf, res_buf, lres_buf, gate_buf, lgate_buf,
    top, weight_sum, blended_buf,
    load_sem, v_sem, kvz_s, kvz_r, qz_s, qz_r, peer_s, peer_r, fr_s, fr_r, fwd_s, fwd_r,
    o_s, o_r, lo_r, res_s, res_r, lres_s, lres_r, gate_s, gate_r, lgate_s, lgate_r, out_sem,
):
    F, Z = frames, heads
    f = lax.axis_index("frame")
    h = lax.axis_index("head")
    t = lax.axis_index("tok")
    T = q_in.shape[0]
    has_prev = f > 0
    has_across = (f > 0) & (f < F - 1)
    partner = f + 1 - 2 * lax.rem(f, 2)
    across = f - 1 + 2 * lax.rem(f, 2)

    def at(fr, hd, tk):
        return {"frame": fr, "head": hd, "tok": tk}

    def remote(src, dst, send, recv, dev):
        return pltpu.make_async_remote_copy(
            src_ref=src, dst_ref=dst, send_sem=send, recv_sem=recv, device_id=dev, device_id_type=MESH
        )

    load_k = pltpu.make_async_copy(k_hbm.at[0], k_in, load_sem.at[0])
    load_q = pltpu.make_async_copy(q_hbm.at[0], q_in, load_sem.at[1])
    load_gate = pltpu.make_async_copy(gate_hbm, gate_in, load_sem.at[2])
    load_v = [
        pltpu.make_async_copy(v_hbm.at[0, :, pl.ds(j * HD, HD)], kv_out.at[j, 1], v_sem.at[j]) for j in range(Z)
    ]
    incoming = pltpu.make_async_copy(inc_hbm, nq_ref.at[0], out_sem)
    load_k.start()
    for c in load_v:
        c.start()
    load_q.start()
    load_gate.start()

    @pl.when(f == F - 1)
    def _():
        incoming.start()

    barrier = pltpu.get_barrier_semaphore()
    me = f * Z + h

    def greet(s, carry):
        other = lax.rem(me + s, F * Z)
        pl.semaphore_signal(barrier, inc=1, device_id=at(other // Z, lax.rem(other, Z), t), device_id_type=MESH)
        return carry

    lax.fori_loop(1, F * Z, greet, 0)
    pl.semaphore_signal(barrier, inc=1, device_id=at(f, h, 1 - t), device_id_type=MESH)

    lane = lax.broadcasted_iota(jnp.int32, (8, HD), 1)
    power = lax.rem(lane, HALF).astype(jnp.float32)
    angle = pos_ref[0].astype(jnp.float32) * jnp.exp2(-power)
    cosine = jnp.where(lane < 2 * HALF, jnp.cos(angle), 1.0)[0:1]
    sine = jnp.sin(angle)
    sine_up = jnp.where(lane < HALF, -sine, 0.0)[0:1]
    sine_down = jnp.where((lane >= HALF) & (lane < 2 * HALF), sine, 0.0)[0:1]

    def turned(x):
        x = x.astype(jnp.float32)
        up = pltpu.roll(x, HD - HALF, 1)
        down = pltpu.roll(x, HALF, 1)
        return (x * cosine + up * sine_up + down * sine_down).astype(jnp.bfloat16)

    load_k.wait()
    for j in range(Z):
        kv_out[j, 0] = turned(k_in[:, j * HD : (j + 1) * HD])
    for c in load_v:
        c.wait()
    pl.semaphore_wait(barrier, F * Z)

    def kv_send(s):
        d = lax.rem(h + s, Z)
        return remote(kv_out.at[d], kv_buf.at[0, t, h], kvz_s.at[s], kvz_r.at[s], at(f, d, t))

    def q_send(s):
        d = lax.rem(h + s, Z)
        return remote(q_out.at[d], q_buf.at[s], qz_s.at[s], qz_r.at[s], at(f, d, t))

    for s in range(1, Z):
        kv_send(s).start()

    def peer_send(s, b, src):
        return remote(src, kv_buf.at[0, t, b], peer_s.at[s], peer_r.at[s], at(f, h, 1 - t))

    def pair_send(s, b, src):
        return remote(src, kv_buf.at[1, t, b], fr_s.at[0, s], fr_r.at[0, s], at(partner, h, t))

    def across_send(s, b, src):
        return remote(src, kv_buf.at[2, t, b], fr_s.at[1, s], fr_r.at[1, s], at(across, h, t))

    def relay_send(s, b):
        return remote(
            kv_buf.at[1, t, b], kv_buf.at[2, t, b], fr_s.at[1, s], fr_r.at[1, s], at(lax.rem(f + 2, F), h, t)
        )

    def fwd_send(slot, s, b):
        ref = kv_buf.at[slot, t, b]
        return remote(ref, ref, fwd_s.at[slot - 1, s], fwd_r.at[slot - 1, s], at(f, h, 1 - t))

    def spread(s, b, src):
        pair_send(s, b, src).start()
        if not relay:

            @pl.when(has_across)
            def _():
                across_send(s, b, src).start()

        peer_send(s, b, src).start()

    spread(0, h, kv_out.at[h])
    load_q.wait()
    for j in range(Z):
        q_out[j] = turned(q_in[:, j * HD : (j + 1) * HD])
    for s in range(1, Z):
        q_send(s).start()
    kv_buf[0, t, h] = kv_out[h]
    q_buf[0] = q_out[h]

    load_gate.wait()
    gate_out[...] = jnp.broadcast_to(gate_in[pl.ds(steps_ref[0], 1), :], gate_out.shape)

    def came(ref, sem):
        remote(ref, ref, sem, sem, at(f, h, 1 - t)).wait_recv()

    def block(s):
        return lax.rem(h + Z - s, Z)

    def take_own(s):
        came(kv_buf.at[0, t, block(s)], kvz_r.at[s])
        spread(s, block(s), kv_buf.at[0, t, block(s)])

    def take_pair(s):
        came(kv_buf.at[1, t, block(s)], fr_r.at[0, s])
        if relay:

            @pl.when(jnp.logical_not(has_across))
            def _():
                relay_send(s, block(s)).start()

        fwd_send(1, s, block(s)).start()

    def take_across(s):
        @pl.when(has_across)
        def _():
            came(kv_buf.at[2, t, block(s)], fr_r.at[1, s])
            fwd_send(2, s, block(s)).start()

    def res_send():
        return remote(res_hbm, res_buf, res_s, res_r, at(f - 1, h, t))

    def gate_send():
        return remote(gate_out, gate_buf, gate_s, gate_r, at(f - 1, h, t))

    def lres_send(g):
        return remote(res_hbm.at[0, :, pl.ds(g * HD, HD)], lres_buf, lres_s.at[g], lres_r, at(g, h, t))

    def lgate_send(g):
        return remote(gate_out.at[:, pl.ds(g * HD, HD)], lgate_buf, lgate_s.at[g], lgate_r, at(g, h, t))

    def send_residual():
        @pl.when(has_prev)
        def _():
            res_send().start()
            gate_send().start()

        @pl.when(f == 0)
        def _():
            pltpu.make_async_copy(res_hbm.at[0, :, pl.ds(0, HD)], lres_buf, lres_r).start()
            pltpu.make_async_copy(gate_out.at[:, pl.ds(0, HD)], lgate_buf, lgate_r).start()
            for g in range(1, F):
                lres_send(g).start()
                lgate_send(g).start()

    for s in range(1, Z):
        take_own(s)
        take_pair(s - 1)
    take_pair(Z - 1)
    send_residual()

    for s in range(Z):
        b = lax.rem(h + s, Z)
        came(kv_buf.at[0, 1 - t, b], peer_r.at[s])

    rate = math.log2(math.e) / math.sqrt(HD)
    keys_all = 2 * Z * T
    group = 2 if Z <= 4 else 1

    def score(rows, slot):
        return lax.dot_general(
            rows,
            kv_buf[slot, :, :, 0].reshape(keys_all, HD),
            (((1,), (1,)), ((), ())),
            preferred_element_type=jnp.float32,
        )

    def blend(weights, slot):
        return jnp.dot(
            weights.astype(jnp.bfloat16),
            kv_buf[slot, :, :, 1].reshape(keys_all, HD),
            preferred_element_type=jnp.float32,
        )

    def near(i, first):
        rows = q_buf[pl.ds(i * group, group)].reshape(group * T, HD)
        own = score(rows, 0)
        if first:
            for s in range(Z):
                b = lax.rem(h + s, Z)
                came(kv_buf.at[1, 1 - t, b], fwd_r.at[0, s])
        beside = score(rows, 1)
        highest = jnp.maximum(jnp.max(own, axis=1, keepdims=True), jnp.max(beside, axis=1, keepdims=True))
        own = jnp.exp2((own - highest) * rate)
        beside = jnp.exp2((beside - highest) * rate)
        at_rows = pl.ds(i * group * T, group * T)
        top[at_rows] = jnp.broadcast_to(highest, (group * T, HD))
        total = jnp.sum(own, axis=1, keepdims=True) + jnp.sum(beside, axis=1, keepdims=True)
        weight_sum[at_rows] = jnp.broadcast_to(total, (group * T, HD))
        blended_buf[at_rows] = blend(own, 0) + blend(beside, 1)

    def take_queries(i):
        for s in range(max(i * group, 1), (i + 1) * group):
            came(q_buf.at[s], qz_r.at[s])

    def finish_across():
        for s in range(Z):
            take_across(s)

        @pl.when(has_across)
        def _():
            for s in range(Z):
                came(kv_buf.at[2, 1 - t, block(s)], fwd_r.at[1, s])

    def o_send(s):
        return remote(o_out.at[s], o_buf.at[h], o_s.at[s], o_r.at[h], at(f - 1, lax.rem(h + Z - s, Z), t))

    def lo_send(s):
        return remote(o_out.at[s], lo_buf, o_s.at[s], lo_r, at(h, lax.rem(h + Z - s, Z), t))

    def leave_with(result, i):
        for g in range(group):
            s = i * group + g
            o_out[s] = result[g * T : (g + 1) * T]

            @pl.when(f > 0)
            def _():
                o_send(s).start()

            @pl.when((f == 0) & ((h != 0) | (s != 0)))
            def _():
                lo_send(s).start()

            @pl.when((f == 0) & (h == 0) & (s == 0))
            def _():
                pltpu.make_async_copy(o_out.at[0], lo_buf, lo_r).start()

    def finish(i, carry):
        at_rows = pl.ds(i * group * T, group * T)

        @pl.when(has_across)
        def _():
            scores = score(q_buf[pl.ds(i * group, group)].reshape(group * T, HD), 2)
            before = top[at_rows]
            highest = jnp.maximum(before, jnp.max(scores, axis=1, keepdims=True))
            keep = jnp.exp2((before - highest) * rate)
            weights = jnp.exp2((scores - highest[:, 0:1]) * rate)
            total = weight_sum[at_rows] * keep + jnp.sum(weights, axis=1, keepdims=True)
            leave_with(((blended_buf[at_rows] * keep + blend(weights, 2)) / total).astype(jnp.bfloat16), i)

        @pl.when(jnp.logical_not(has_across))
        def _():
            leave_with((blended_buf[at_rows] / weight_sum[at_rows]).astype(jnp.bfloat16), i)

        return carry

    if Z <= 4:
        for i in range(Z // group):
            take_queries(i)
            near(i, i == 0)
        finish_across()
        for i in range(Z // group):
            finish(i, 0)
    else:
        for i in range(Z // group):
            take_queries(i)
        near(0, True)
        finish_across()
        lax.fori_loop(1, Z // group, lambda i, c: (near(i, False), c)[1], 0)
        lax.fori_loop(0, Z // group, finish, 0)

    came(lres_buf, lres_r)
    came(lgate_buf, lgate_r)
    came(lo_buf, lo_r)
    lv_ref[...] = (
        lres_buf[...].astype(jnp.float32) + lgate_buf[0:1, :] * lo_buf[...].astype(jnp.float32)
    ).astype(jnp.bfloat16)

    @pl.when(f < F - 1)
    def _():
        came(res_buf, res_r)
        came(gate_buf, gate_r)
        for j in range(Z):
            came(o_buf.at[j], o_r.at[j])
            cols = slice(j * HD, (j + 1) * HD)
            nq_ref[0, :, cols] = (
                res_buf[0, :, cols].astype(jnp.float32) + gate_buf[0:1, cols] * o_buf[j].astype(jnp.float32)
            ).astype(jnp.bfloat16)

    @pl.when(f == F - 1)
    def _():
        incoming.wait()

    for s in range(Z):
        if s > 0:
            kv_send(s).wait_send()
            q_send(s).wait_send()
        peer_send(s, 0, kv_out.at[0]).wait_send()
        pair_send(s, 0, kv_out.at[0]).wait_send()
        fwd_send(1, s, 0).wait_send()

        @pl.when(has_across)
        def _():
            fwd_send(2, s, 0).wait_send()

        if relay:

            @pl.when(jnp.logical_not(has_across))
            def _():
                relay_send(s, 0).wait_send()

        else:

            @pl.when(has_across)
            def _():
                across_send(s, 0, kv_out.at[0]).wait_send()

        @pl.when((f > 0) | (h != 0) | (s != 0))
        def _():
            o_send(s).wait_send()

    @pl.when(has_prev)
    def _():
        res_send().wait_send()
        gate_send().wait_send()

    @pl.when(f == 0)
    def _():
        for g in range(1, F):
            lres_send(g).wait_send()
            lgate_send(g).wait_send()


def solution(mesh):
    F, Z = mesh.shape["frame"], mesh.shape["head"]

    def per_device(queries, keys, values, residual, incoming, gate_table, timesteps, positions):
        T, HH = queries.shape[1], queries.shape[2]
        assert HH == Z * HD and HH == F * HD and mesh.shape["tok"] == 2
        blocks = (queries, keys, values, residual, incoming, gate_table)
        bf, f32 = jnp.bfloat16, jnp.float32
        dma = pltpu.SemaphoreType.DMA
        anywhere = pl.BlockSpec(memory_space=pl.ANY)
        smem = pl.BlockSpec(memory_space=pltpu.SMEM)
        return pl.pallas_call(
            functools.partial(kernel, F, Z, F == 4),
            out_shape=(
                jax.ShapeDtypeStruct((1, T, HH), bf),
                jax.ShapeDtypeStruct((T, HD), bf),
            ),
            in_specs=[anywhere] * 6 + [smem, smem],
            out_specs=(pl.BlockSpec(memory_space=pltpu.VMEM),) * 2,
            scratch_shapes=[
                pltpu.VMEM((T, HH), bf),
                pltpu.VMEM((T, HH), bf),
                pltpu.VMEM(gate_table.shape, f32),
                pltpu.VMEM((Z, 2, T, HD), bf),
                pltpu.VMEM((Z, T, HD), bf),
                pltpu.VMEM((8, HH), f32),
                pltpu.VMEM((3, 2, Z, 2, T, HD), bf),
                pltpu.VMEM((Z, T, HD), bf),
                pltpu.VMEM((Z, T, HD), bf),
                pltpu.VMEM((Z, T, HD), bf),
                pltpu.VMEM((T, HD), bf),
                pltpu.VMEM((1, T, HH), bf),
                pltpu.VMEM((T, HD), bf),
                pltpu.VMEM((8, HH), f32),
                pltpu.VMEM((8, HD), f32),
                pltpu.VMEM((Z * T, HD), f32),
                pltpu.VMEM((Z * T, HD), f32),
                pltpu.VMEM((Z * T, HD), f32),
                dma((3,)), dma((Z,)),
                dma((Z,)), dma((Z,)), dma((Z,)), dma((Z,)),
                dma((Z,)), dma((Z,)), dma((2, Z)), dma((2, Z)), dma((2, Z)), dma((2, Z)),
                dma((Z,)), dma((Z,)), dma,
                dma, dma, dma((F,)), dma,
                dma, dma, dma((F,)), dma,
                dma,
            ],
            compiler_params=pltpu.CompilerParams(
                collective_id=0, has_side_effects=True, vmem_limit_bytes=48 * 1024 * 1024
            ),
        )(
            *(pltpu.with_memory_space_constraint(x, pltpu.HBM) for x in blocks), timesteps, positions
        )

    placed = (
        P("frame", ("head", "tok"), None),
        P("frame", ("head", "tok"), None),
        P("frame", ("head", "tok"), None),
        P("frame", ("head", "tok"), None),
        P(("head", "tok"), None),
        P(),
        P("frame"),
        P("frame"),
    )
    return jax.shard_map(
        per_device,
        mesh=mesh,
        in_specs=placed,
        out_specs=(P("frame", ("head", "tok"), None), P(("head", "tok"), "frame")),
        check_vma=False,
    )
```
